512 devices in a mesh: head: 8 (over z_lo), query: 2 (over z_hi), slot: 32 (over x, y, core).
Axes of the slice: x: 4, y: 4, z: 16 (z_hi: 2, z_lo: 8; z = z_hi * 8 + z_lo), core: 2. Of those that a mesh axis runs over, the one named last changes fastest.
Arguments:
- queries: bfloat16 [8, 4096, 128], P('head', 'query'), may hold values from -128 to 128
- keys: bfloat16 [8, 32768, 128], P('head', 'slot'), may hold values from -4 to 4
- values: bfloat16 [8, 32768, 128], P('head', 'slot'), may hold values from -5 to 5
- bias: float32 [8, 32768], P('head', 'slot'), may hold values from -4 to 4
- targets: float32 [8, 4096, 128], P('head', 'query'), may hold values from -0.3 to 0.3
- target_lse: float32 [8, 4096], P('head', 'query'), may hold values from 9 to 12
Outputs:
- step_keys: float32 [8, 32768, 128], P('head', 'slot')
- step_values: float32 [8, 32768, 128], P('head', 'slot')
- step_bias: float32 [8, 32768], P('head', 'slot')
The draws below stay inside these ranges and needn't reach their ends.
All inputs are finite; a program needn't handle non-finite values.
Results may differ from the reference program's by a relative error of at most 0.015.
Values sent between devices are 32-bit elements; how exact they have to be, the bound alone decides.
No kernel may reach another device: no remote copies, remote signals or barrier semaphores. Data moves between devices by JAX's collectives and lax.ppermute only.
A program may use at most 128 MiB of HBM per device.

```python
import jax
import jax.numpy as jnp
from jax import lax

H = 8
DH = 128
S = 32768
R = 4096


def drawn_slots(key):
    width = S // 8
    offsets = jax.random.randint(jax.random.fold_in(key, 11), (H, 8), 0, width - 1)
    return jnp.arange(8, dtype=jnp.int32)[None, :] * width + offsets


def shared_keys(key):
    base = jnp.clip(jax.random.normal(jax.random.fold_in(key, 13), (H, S, DH), jnp.float32), -4.0, 4.0)
    slots = drawn_slots(key)
    heads = jnp.broadcast_to(jnp.arange(H, dtype=jnp.int32)[:, None], (H, 8))
    current = base[heads, slots + 1]
    mixed = current
    return base.at[heads, slots + 1].set(mixed)


def draw_keys(key, part):
    keys_all = shared_keys(key)
    return keys_all.astype(jnp.bfloat16)


def draw_queries(key, part):
    key = jax.random.fold_in(key, 5)
    drawn = jnp.clip(jax.random.normal(key, (H, R, DH), jnp.float32), -4.0, 4.0)
    return drawn.astype(jnp.bfloat16)


def steps_of(key, dims, pieces, least, top_value):
    def one(position, blocks):
        draws = jax.random.uniform(jax.random.fold_in(jax.random.fold_in(key, 6), position), (blocks,), jnp.float32, least / len(pieces), top_value / len(pieces))
        return jnp.repeat(jnp.exp(draws), dims[position] // blocks).reshape((-1,) + (1,) * (len(dims) - position - 1))

    loudness = one(*pieces[0])
    for cut in pieces[1:]:
        loudness = loudness * one(*cut)
    return loudness


def scatter_about(own_key, extent, scale, most, pieces=(), held_as=jnp.bfloat16):
    factor_of = steps_of(own_key, extent, pieces, -0.22, 0.18) if pieces else 1.0
    values = jax.random.normal(own_key, extent, jnp.float32) * scale * factor_of
    return jnp.minimum(jnp.maximum(values, -most), most).astype(held_as)


def setup_inputs(seed: int = 0) -> dict:
    streams_of = jax.random.split(jax.random.key(seed), 7)
    queries = draw_queries(jax.random.fold_in(streams_of[6], 71), 0)
    keys = draw_keys(jax.random.fold_in(streams_of[6], 71), 0)
    values = scatter_about(streams_of[2], (H, S, DH), 1.0, 5.0, ((0, 8), (1, 32)))
    bias = scatter_about(streams_of[3], (H, S), 1.0, 4.0, ((0, 8), (1, 32)), jnp.float32)
    targets = scatter_about(streams_of[4], (H, R, DH), 0.05, 0.3, ((0, 8), (1, 2)), jnp.float32)
    target_lse = jnp.clip(9.0 + 3.0 * jax.random.uniform(streams_of[5], (H, R), jnp.float32) ** steps_of(streams_of[5], (H, R), ((0, 8), (1, 2)), -0.2, 0.2), 9.0, 12.0)
    return dict(queries=queries, keys=keys, values=values, bias=bias, targets=targets, target_lse=target_lse)


EPS = 1e-06

def head_grads(operands):
    q, k, v, b, y, t = operands
    scale = DH ** (-0.5)
    blk = min(512, R)
    nb = R // blk
    qs = q.reshape(nb, blk, DH)
    ys = y.reshape(nb, blk, DH)
    ts = t.reshape(nb, blk)

    def step(carry, xs):
        gk, gv, gb = carry
        qb, yb, tb = xs
        s = jnp.dot(qb, k.T, preferred_element_type=jnp.float32) * scale + b[None, :]
        top = lax.optimization_barrier(jnp.max(s, axis=1, keepdims=True))
        e = jnp.exp(s - top)
        tot = lax.optimization_barrier(jnp.sum(e, axis=1, keepdims=True))
        o = jnp.dot(e.astype(jnp.bfloat16), v, preferred_element_type=jnp.float32) / tot
        lse = top[:, 0] + jnp.log(tot[:, 0])
        go = o - yb
        gl = lse - tb
        gob = go.astype(jnp.bfloat16)
        p = e / tot
        dp = jnp.dot(gob, v.T, preferred_element_type=jnp.float32)
        ds = p * (dp - lax.optimization_barrier(jnp.sum(go * o, axis=1, keepdims=True)) + gl[:, None])
        gv = gv + jnp.dot(p.astype(jnp.bfloat16).T, gob, preferred_element_type=jnp.float32)
        gb = gb + lax.optimization_barrier(jnp.sum(ds, axis=0))
        gk = gk + jnp.dot(ds.astype(jnp.bfloat16).T, qb, preferred_element_type=jnp.float32) * scale
        return ((gk, gv, gb), None)
    init = (jnp.zeros((S, DH), jnp.float32), jnp.zeros((S, DH), jnp.float32), jnp.zeros((S,), jnp.float32))
    out, _ = lax.scan(step, init, (qs, ys, ts))
    return out

def normalize(grad):
    return grad / jnp.sqrt(jnp.mean(grad * grad) + EPS)

def reference(queries, keys, values, bias, targets, target_lse):
    gk, gv, gb = lax.map(head_grads, (queries, keys, values, bias, targets, target_lse))
    return (normalize(gk), normalize(gv), normalize(gb))
```

```python
import functools
import math

import jax
import jax.numpy as jnp
from jax import lax
from jax.experimental import pallas as pl
from jax.experimental.pallas import tpu as pltpu
from jax.sharding import PartitionSpec as P

EPS = 1e-06
LOG2E = math.log2(math.e)
F32 = jnp.float32
BF16 = jnp.bfloat16
VMEM_BYTES = 48 * 1024 * 1024
STAT = 8
ROWS = 256


def params():
    return pltpu.CompilerParams(vmem_limit_bytes=VMEM_BYTES)


def whole():
    return pl.BlockSpec(memory_space=pltpu.VMEM)


def contract(a, b, dims):
    return lax.dot_general(a, b, ((dims[:1], dims[1:]), ((), ())), preferred_element_type=F32)


def spread_bias(bias_ref, out_ref):
    slots = bias_ref.shape[1]
    out_ref[...] = jnp.broadcast_to(bias_ref[...] * LOG2E, (128, slots)).T


def tiled_lanes(x, times):
    return jnp.concatenate([x] * times, axis=1)


def forward_kernel(scale, q_ref, k_ref, v_ref, bias_ref, out_ref, bias_s, vt_s):
    rows, dim = q_ref.shape
    half = dim // 2
    spread_bias(bias_ref, bias_s)
    vt_s[...] = v_ref[...].T
    for r in range(rows // ROWS):
        q = q_ref[r * ROWS : (r + 1) * ROWS, :]
        s = contract(k_ref[...], q, (1, 1)) * (scale * LOG2E) + tiled_lanes(bias_s[...], ROWS // 128)
        top = jnp.max(s, axis=0, keepdims=True)
        e = jnp.exp2(s - top)
        total = jnp.sum(e, axis=0, keepdims=True)
        o = contract(vt_s[...], e.astype(BF16), (1, 0))
        for g in range(ROWS // 128):
            block = r * (ROWS // 128) + g
            lanes = slice(g * 128, (g + 1) * 128)
            for c in range(2):
                out_ref[2 * block + c, :half, :] = o[c * half : (c + 1) * half, lanes]
                out_ref[2 * block + c, half : half + 1, :] = top[:, lanes]
                out_ref[2 * block + c, half + 1 : half + 2, :] = total[:, lanes]


def combine_kernel(place_ref, got_ref, t_ref, tl_ref, out_ref, t_s):
    n = got_ref.shape[0]
    half = got_ref.shape[1] - STAT
    core = place_ref[1]
    tops = got_ref[:, half, :]
    totals = got_ref[:, half + 1, :]
    top = jnp.max(tops, axis=0, keepdims=True)
    factor = jnp.exp2(tops - top)
    total = jnp.sum(totals * factor, axis=0, keepdims=True)
    summed = got_ref[0, :half, :] * factor[0:1, :]
    for i in range(1, n):
        summed += got_ref[i, :half, :] * factor[i : i + 1, :]
    outputs = summed / total
    lse2 = top + jnp.log2(total)
    t_s[...] = t_ref[...].T
    start = pl.multiple_of(core * half, half)
    grad_out = outputs - t_s[pl.ds(start, half), :]
    grad_lse = lse2 * math.log(2.0) - tl_ref[pl.ds(place_ref[0], 1), :]
    part = jnp.sum(grad_out * outputs, axis=0, keepdims=True)
    first = jnp.where(core == 0, 1.0, 0.0).astype(F32)
    out_ref[:half, :] = grad_out
    out_ref[half : half + 1, :] = lse2
    out_ref[half + 1 : half + 2, :] = part - first * grad_lse
    out_ref[half + 2 :, :] = jnp.zeros((STAT - 2, 128), F32)


def backward_rows(scale, r, q_ref, g_ref, k_ref, v_ref, bias_s):
    half = g_ref.shape[1] - STAT
    pieces, lses, shifts = [], [], []
    for g in range(ROWS // 128):
        block = r * (ROWS // 128) + g
        pieces.append(
            jnp.concatenate([g_ref[2 * block, :half, :], g_ref[2 * block + 1, :half, :]], axis=0)
        )
        lses.append(g_ref[2 * block, half : half + 1, :])
        shifts.append(
            g_ref[2 * block, half + 1 : half + 2, :] + g_ref[2 * block + 1, half + 1 : half + 2, :]
        )
    grad_out = jnp.concatenate(pieces, axis=1).astype(BF16)
    lse2 = jnp.concatenate(lses, axis=1)
    shift = jnp.concatenate(shifts, axis=1)
    q = q_ref[r * ROWS : (r + 1) * ROWS, :]
    s = contract(k_ref[...], q, (1, 1)) * (scale * LOG2E) + tiled_lanes(bias_s[...], ROWS // 128)
    p = jnp.exp2(s - lse2)
    inner = contract(v_ref[...], grad_out, (1, 0))
    d = p * (inner - shift)
    gv = contract(p.astype(BF16), grad_out, (1, 1))
    gk = contract(d.astype(BF16), q, (1, 0))
    gb = d[:, :128]
    for g in range(1, ROWS // 128):
        gb = gb + d[:, g * 128 : (g + 1) * 128]
    return gk, gv, gb


def backward_kernel(scale, q_ref, g_ref, k_ref, v_ref, bias_ref, gk_ref, gv_ref, gb_ref, bias_s):
    spread_bias(bias_ref, bias_s)
    for r in range(q_ref.shape[0] // ROWS):
        gk, gv, gb = backward_rows(scale, r, q_ref, g_ref, k_ref, v_ref, bias_s)
        if r == 0:
            gk_ref[...], gv_ref[...], gb_ref[...] = gk, gv, gb
        else:
            gk_ref[...] += gk
            gv_ref[...] += gv
            gb_ref[...] += gb


def finish_kernel(
    scale, place_ref, qa_ref, qb_ref, g_ref, k_ref, v_ref, bias_ref, gk0_ref, gv0_ref, gb0_ref,
    gk_ref, gv_ref, gb_ref, sq_ref, bias_s, gb_s, q_ref
):
    spread_bias(bias_ref, bias_s)
    part = qa_ref.shape[0]
    core = place_ref[1]
    q_ref[pl.ds(pl.multiple_of(core * part, part), part), :] = qa_ref[...].astype(BF16)
    q_ref[pl.ds(pl.multiple_of((1 - core) * part, part), part), :] = qb_ref[...].astype(BF16)
    gk_ref[...] = gk0_ref[...]
    gv_ref[...] = gv0_ref[...]
    gb_s[...] = gb0_ref[...]
    for r in range(q_ref.shape[0] // ROWS):
        gk, gv, gb = backward_rows(scale, r, q_ref, g_ref, k_ref, v_ref, bias_s)
        gk_ref[...] += gk
        gv_ref[...] += gv
        gb_s[...] += gb
    gk = gk_ref[...] * scale
    gk_ref[...] = gk
    gv = gv_ref[...]
    gb = jnp.sum(gb_s[...].T, axis=0, keepdims=True)
    gb_ref[...] = gb
    lane = lax.broadcasted_iota(jnp.int32, (1, 128), 1)
    sums = [jnp.sum(x * x) for x in (gk, gv, gb)]
    sq_ref[...] = jnp.where(lane == 0, sums[0], jnp.where(lane == 1, sums[1], sums[2]))


def scale_kernel(counts, sq_ref, gk_ref, gv_ref, gb_ref, ok_ref, ov_ref, ob_ref):
    total = jnp.sum(sq_ref[...], axis=0, keepdims=True)
    lane = lax.broadcasted_iota(jnp.int32, (1, 128), 1)
    refs = ((gk_ref, ok_ref), (gv_ref, ov_ref), (gb_ref, ob_ref))
    for i, ((g_ref, o_ref), count) in enumerate(zip(refs, counts)):
        mean = jnp.sum(jnp.where(lane == i, total, 0.0), axis=1, keepdims=True) / count
        o_ref[...] = g_ref[...] * (1.0 / jnp.sqrt(mean + EPS))


def local(queries, keys, values, bias, targets, target_lse):
    q, k, v, t = queries[0], keys[0], values[0], targets[0]
    rows, dim = q.shape
    slots = k.shape[0]
    half = dim // 2
    scale = dim ** (-0.5)
    n_slot = lax.axis_size("slot")
    n_head = lax.axis_size("head")
    me = lax.axis_index("slot")
    block, core = me // 2, me % 2
    swap = [(0, 1), (1, 0)]

    own = lax.dynamic_slice_in_dim(q, core * (rows // 2), rows // 2, 0).astype(F32)
    far = lax.ppermute(own, "query", swap)
    far_other = lax.ppermute(far, "slot", [(i, i ^ 1) for i in range(n_slot)])
    place = jnp.stack([block, core]).astype(jnp.int32)

    parts = pl.pallas_call(
        functools.partial(forward_kernel, scale),
        out_shape=jax.ShapeDtypeStruct((n_slot, half + STAT, 128), F32),
        in_specs=[whole()] * 4,
        out_specs=whole(),
        scratch_shapes=[pltpu.VMEM((slots, 128), F32), pltpu.VMEM((dim, slots), BF16)],
        compiler_params=params(),
        name="forward",
    )(q, k, v, bias)
    got = lax.all_to_all(parts, "slot", 0, 0)
    mine = pl.pallas_call(
        combine_kernel,
        out_shape=jax.ShapeDtypeStruct((half + STAT, 128), F32),
        grid_spec=pltpu.PrefetchScalarGridSpec(
            num_scalar_prefetch=1,
            grid=(1,),
            in_specs=[
                pl.BlockSpec((n_slot, half + STAT, 128), lambda i, p: (0, 0, 0)),
                pl.BlockSpec((128, dim), lambda i, p: (p[0], 0)),
                pl.BlockSpec((rows // 128, 128), lambda i, p: (0, 0)),
            ],
            out_specs=pl.BlockSpec((half + STAT, 128), lambda i, p: (0, 0)),
            scratch_shapes=[pltpu.VMEM((dim, 128), F32)],
        ),
        compiler_params=params(),
        name="combine",
    )(place, got, t, target_lse.reshape(rows // 128, 128))

    def spread(x):
        return lax.all_to_all(jnp.broadcast_to(x[None], (n_slot,) + x.shape), "slot", 0, 0)

    theirs = lax.ppermute(mine, "query", swap)
    near = spread(mine)
    away = spread(theirs)
    flops = 8 * rows * slots * dim
    cost = pl.CostEstimate(flops=flops, bytes_accessed=4 << 20, transcendentals=rows * slots)
    mat = jax.ShapeDtypeStruct((slots, dim), F32)
    wide = jax.ShapeDtypeStruct((slots, 128), F32)
    gk, gv, gb = pl.pallas_call(
        functools.partial(backward_kernel, scale),
        out_shape=(mat, mat, wide),
        in_specs=[whole()] * 5,
        out_specs=(whole(),) * 3,
        scratch_shapes=[pltpu.VMEM((slots, 128), F32)],
        compiler_params=params(),
        cost_estimate=cost,
        name="backward_near",
    )(q, near, k, v, bias)
    gk, gv, gb, sq = pl.pallas_call(
        functools.partial(finish_kernel, scale),
        out_shape=(mat, mat, jax.ShapeDtypeStruct((1, slots), F32), jax.ShapeDtypeStruct((1, 128), F32)),
        in_specs=[pl.BlockSpec(memory_space=pltpu.SMEM)] + [whole()] * 9,
        out_specs=(whole(),) * 4,
        scratch_shapes=[
            pltpu.VMEM((slots, 128), F32),
            pltpu.VMEM((slots, 128), F32),
            pltpu.VMEM((rows, dim), BF16),
        ],
        compiler_params=params(),
        cost_estimate=cost,
        name="backward_far",
    )(place, far, far_other, away, k, v, bias, gk, gv, gb)
    n_all = n_head * n_slot
    sq_all = lax.all_to_all(jnp.broadcast_to(sq[None], (n_all, 1, 128)), ("head", "slot"), 0, 0)
    counts = (float(n_all * slots * dim), float(n_all * slots * dim), float(n_all * slots))
    ok, ov, ob = pl.pallas_call(
        functools.partial(scale_kernel, counts),
        out_shape=(mat, mat, jax.ShapeDtypeStruct((1, slots), F32)),
        in_specs=[whole()] * 4,
        out_specs=(whole(),) * 3,
        compiler_params=params(),
        name="normalize",
    )(sq_all.reshape(n_all, 128), gk, gv, gb)
    return ok[None], ov[None], ob


def solution(mesh):
    placed = (
        P("head", "query", None),
        P("head", "slot", None),
        P("head", "slot", None),
        P("head", "slot"),
        P("head", "query", None),
        P("head", "query"),
    )
    return jax.shard_map(
        local,
        mesh=mesh,
        in_specs=placed,
        out_specs=(P("head", "slot", None), P("head", "slot", None), P("head", "slot")),
        check_vma=False,
    )
```

```python
import functools
import math

import jax
import jax.numpy as jnp
from jax import lax
from jax.experimental import pallas as pl
from jax.experimental.pallas import tpu as pltpu
from jax.sharding import PartitionSpec as P

EPS = 1e-06
LOG2E = math.log2(math.e)
F32 = jnp.float32
BF16 = jnp.bfloat16
MIB = 1024 * 1024
STAT = 8
ROWS = 256


def params(mib):
    return pltpu.CompilerParams(vmem_limit_bytes=mib * MIB)


def whole(shape):
    return pl.BlockSpec(shape, lambda *_: (0,) * len(shape))


def call(kernel, outs, scratch, place, *args, cost=None, mib=32, name=None):
    return pl.pallas_call(
        kernel,
        out_shape=[jax.ShapeDtypeStruct(o, F32) for o in outs],
        grid_spec=pltpu.PrefetchScalarGridSpec(
            num_scalar_prefetch=1,
            grid=(1,),
            in_specs=[whole(a.shape) for a in args],
            out_specs=[whole(o) for o in outs],
            scratch_shapes=scratch,
        ),
        compiler_params=params(mib),
        cost_estimate=cost,
        name=name,
    )(place, *args)


def contract(a, b, dims):
    return lax.dot_general(a, b, ((dims[:1], dims[1:]), ((), ())), preferred_element_type=F32)


def spread_bias(bias_ref, out_ref):
    slots = bias_ref.shape[1]
    out_ref[...] = jnp.broadcast_to(bias_ref[...] * LOG2E, (128, slots)).T


def tiled_lanes(x, times):
    return jnp.concatenate([x] * times, axis=1)


def forward_kernel(scale, place_ref, q_ref, k_ref, v_ref, bias_ref, out_ref, bias_s, vt_s):
    rows, dim = q_ref.shape
    half = dim // 2
    spread_bias(bias_ref, bias_s)
    vt_s[...] = v_ref[...].T
    for r in range(rows // ROWS):
        q = q_ref[r * ROWS : (r + 1) * ROWS, :]
        s = contract(k_ref[...], q, (1, 1)) * (scale * LOG2E) + tiled_lanes(bias_s[...], ROWS // 128)
        top = jnp.max(s, axis=0, keepdims=True)
        e = jnp.exp2(s - top)
        total = jnp.sum(e, axis=0, keepdims=True)
        o = contract(vt_s[...], e.astype(BF16), (1, 0))
        for g in range(ROWS // 128):
            block = r * (ROWS // 128) + g
            lanes = slice(g * 128, (g + 1) * 128)
            for c in range(2):
                out_ref[2 * block + c, :half, :] = o[c * half : (c + 1) * half, lanes]
                out_ref[2 * block + c, half : half + 1, :] = top[:, lanes]
                out_ref[2 * block + c, half + 1 : half + 2, :] = total[:, lanes]


def combine_kernel(place_ref, got_ref, t_ref, tl_ref, far_ref, out_ref, all_ref, t_s):
    n = got_ref.shape[0]
    half = got_ref.shape[1] - STAT
    core = place_ref[1]
    tops = got_ref[:, half, :]
    totals = got_ref[:, half + 1, :]
    top = jnp.max(tops, axis=0, keepdims=True)
    factor = jnp.exp2(tops - top)
    total = jnp.sum(totals * factor, axis=0, keepdims=True)
    summed = got_ref[0, :half, :] * factor[0:1, :]
    for i in range(1, n):
        summed += got_ref[i, :half, :] * factor[i : i + 1, :]
    outputs = summed / total
    lse2 = top + jnp.log2(total)
    t_s[...] = t_ref[...].T
    start = pl.multiple_of(core * half, half)
    grad_out = outputs - t_s[pl.ds(start, half), :]
    grad_lse = lse2 * math.log(2.0) - tl_ref[pl.ds(place_ref[0], 1), :]
    part = jnp.sum(grad_out * outputs, axis=0, keepdims=True)
    first = jnp.where(core == 0, 1.0, 0.0).astype(F32)
    out_ref[:half, :] = grad_out
    out_ref[half : half + 1, :] = lse2
    out_ref[half + 1 : half + 2, :] = part - first * grad_lse
    out_ref[half + 2 :, :] = jnp.zeros((STAT - 2, 128), F32)
    mine = out_ref[...]
    far = far_ref[...]
    for i in range(all_ref.shape[0]):
        all_ref[i, : half + STAT, :] = mine
        all_ref[i, half + STAT :, :] = far


def gather_rows(core, ga_ref, gb_ref, half, grad_s):
    n = ga_ref.shape[0]
    for b in range(n):
        lanes = slice(b * 128, (b + 1) * 128)
        grad_s[pl.ds(pl.multiple_of(core * half, half), half), lanes] = ga_ref[b, :half, :].astype(BF16)
        grad_s[pl.ds(pl.multiple_of((1 - core) * half, half), half), lanes] = gb_ref[b, :half, :].astype(BF16)


def backward_rows(scale, r, q_ref, ga_ref, gb_ref, k_ref, v_ref, bias_s, grad_s):
    half = k_ref.shape[1] // 2
    blocks = range(r * (ROWS // 128), (r + 1) * (ROWS // 128))
    lse2 = jnp.concatenate([ga_ref[b, half : half + 1, :] for b in blocks], axis=1)
    shift = jnp.concatenate(
        [ga_ref[b, half + 1 : half + 2, :] + gb_ref[b, half + 1 : half + 2, :] for b in blocks], axis=1
    )
    grad_out = grad_s[:, r * ROWS : (r + 1) * ROWS]
    q = q_ref[r * ROWS : (r + 1) * ROWS, :]
    s = contract(k_ref[...], q, (1, 1)) * (scale * LOG2E) + tiled_lanes(bias_s[...], ROWS // 128)
    p = jnp.exp2(s - lse2)
    inner = contract(v_ref[...], grad_out, (1, 0))
    d = p * (inner - shift)
    gv = contract(p.astype(BF16), grad_out, (1, 1))
    gk = contract(d.astype(BF16), q, (1, 0))
    gb = d[:, :128]
    for g in range(1, ROWS // 128):
        gb = gb + d[:, g * 128 : (g + 1) * 128]
    return gk, gv, gb


def near_kernel(
    scale, place_ref, q_ref, ga_ref, gb_ref, k_ref, v_ref, bias_ref, gk_ref, gv_ref, gb_out_ref, bias_s, grad_s
):
    spread_bias(bias_ref, bias_s)
    gather_rows(place_ref[1], ga_ref, gb_ref, k_ref.shape[1] // 2, grad_s)
    for r in range(q_ref.shape[0] // ROWS):
        gk, gv, gb = backward_rows(scale, r, q_ref, ga_ref, gb_ref, k_ref, v_ref, bias_s, grad_s)
        if r == 0:
            gk_ref[...], gv_ref[...], gb_out_ref[...] = gk, gv, gb
        else:
            gk_ref[...] += gk
            gv_ref[...] += gv
            gb_out_ref[...] += gb


def far_kernel(
    scale, place_ref, qa_ref, qb_ref, ga_ref, gb_ref, k_ref, v_ref, bias_ref, gk0_ref, gv0_ref, gb0_ref,
    gk_ref, gv_ref, gb_out_ref, sq_ref, bias_s, grad_s, gb_s, q_s
):
    core = place_ref[1]
    half = k_ref.shape[1] // 2
    spread_bias(bias_ref, bias_s)
    gather_rows(core, ga_ref, gb_ref, half, grad_s)
    skip = half + STAT
    for b in range(qa_ref.shape[0]):
        q_s[pl.ds(pl.multiple_of(b * 128 + core * 64, 64), 64), :] = qa_ref[b, skip:, :].astype(BF16)
        q_s[pl.ds(pl.multiple_of(b * 128 + (1 - core) * 64, 64), 64), :] = qb_ref[b, skip:, :].astype(BF16)
    gk_ref[...] = gk0_ref[...]
    gv_ref[...] = gv0_ref[...]
    gb_s[...] = gb0_ref[...]
    for r in range(q_s.shape[0] // ROWS):
        gk, gv, gb = backward_rows(scale, r, q_s, ga_ref, gb_ref, k_ref, v_ref, bias_s, grad_s)
        gk_ref[...] += gk
        gv_ref[...] += gv
        gb_s[...] += gb
    gk = gk_ref[...] * scale
    gk_ref[...] = gk
    gv = gv_ref[...]
    gb = jnp.sum(gb_s[...].T, axis=0, keepdims=True)
    gb_out_ref[...] = gb
    lane = lax.broadcasted_iota(jnp.int32, (1, 128), 1)
    sums = [jnp.sum(x * x) for x in (gk, gv, gb)]
    row = jnp.where(lane == 0, sums[0], jnp.where(lane == 1, sums[1], sums[2]))
    sq_ref[...] = jnp.broadcast_to(row, sq_ref.shape)


def scale_kernel(counts, place_ref, sq_ref, gk_ref, gv_ref, gb_ref, ok_ref, ov_ref, ob_ref):
    total = jnp.sum(sq_ref[...], axis=0, keepdims=True)
    lane = lax.broadcasted_iota(jnp.int32, (1, 128), 1)
    refs = ((gk_ref, ok_ref), (gv_ref, ov_ref), (gb_ref, ob_ref))
    for i, ((g_ref, o_ref), count) in enumerate(zip(refs, counts)):
        mean = jnp.sum(jnp.where(lane == i, total, 0.0), axis=1, keepdims=True) / count
        o_ref[...] = g_ref[...] * (1.0 / jnp.sqrt(mean + EPS))


def local(queries, keys, values, bias, targets, target_lse):
    q, k, v, t = queries[0], keys[0], values[0], targets[0]
    rows, dim = q.shape
    slots = k.shape[0]
    half = dim // 2
    scale = dim ** (-0.5)
    n_chip = lax.axis_size("chip")
    n_slot = 2 * n_chip
    n_all = lax.axis_size("head") * n_slot
    chip, core = lax.axis_index("chip"), lax.axis_index("core")
    place = jnp.stack([chip, core]).astype(jnp.int32)
    across = [(0, 1), (1, 0)]
    wide = pltpu.VMEM((slots, 128), F32)

    (parts,) = call(
        functools.partial(forward_kernel, scale),
        [(n_slot, half + STAT, 128)],
        [wide, pltpu.VMEM((dim, slots), BF16)],
        place, q, k, v, bias, mib=62, name="forward",
    )
    parts, q_later = lax.optimization_barrier((parts, q))
    got = lax.all_to_all(parts, ("chip", "core"), 0, 0)
    own = lax.dynamic_slice_in_dim(q_later, (chip * 2 + core) * 64, 64, 0).astype(F32)
    far = lax.ppermute(own, "query", across)
    t_own = lax.dynamic_slice_in_dim(t, chip * 128, 128, 0)
    mine, spread = call(
        combine_kernel,
        [(half + STAT, 128), (n_chip, half + STAT + 64, 128)],
        [pltpu.VMEM((dim, 128), F32)],
        place, got, t_own, target_lse.reshape(rows // 128, 128), far, name="combine",
    )

    def trade(x):
        return lax.all_to_all(x, "chip", 0, 0)

    near_a = trade(spread)
    theirs = lax.ppermute(mine, "query", across)
    near_a, theirs = lax.optimization_barrier((near_a, theirs))
    near_b = lax.ppermute(near_a, "core", across)
    far_a = trade(jnp.broadcast_to(theirs[None], (n_chip,) + theirs.shape))
    cost = pl.CostEstimate(flops=8 * rows * slots * dim, bytes_accessed=4 << 20, transcendentals=rows * slots)
    grad_s = pltpu.VMEM((dim, rows), BF16)
    mat = (slots, dim)
    gk, gv, gb = call(
        functools.partial(near_kernel, scale),
        [mat, mat, (slots, 128)],
        [wide, grad_s],
        place, q, near_a, near_b, k, v, bias, cost=cost, mib=62, name="backward_near",
    )
    far_a, gk, gv, gb = lax.optimization_barrier((far_a, gk, gv, gb))
    far_b = lax.ppermute(far_a, "core", across)
    gk, gv, gb, sq = call(
        functools.partial(far_kernel, scale),
        [mat, mat, (1, slots), (n_all, 128)],
        [wide, grad_s, wide, pltpu.VMEM((rows, dim), BF16)],
        place, near_a, near_b, far_a, far_b, k, v, bias, gk, gv, gb, cost=cost, mib=62, name="backward_far",
    )
    sq_all = lax.all_to_all(sq.reshape(n_all, 1, 128), ("head", "chip", "core"), 0, 0)
    counts = (float(n_all * slots * dim), float(n_all * slots * dim), float(n_all * slots))
    ok, ov, ob = call(
        functools.partial(scale_kernel, counts),
        [mat, mat, (1, slots)],
        [],
        place, sq_all.reshape(n_all, 128), gk, gv, gb, mib=62, name="normalize",
    )
    return ok[None], ov[None], ob


def solution(mesh):
    heads, halves, slots = (mesh.shape[name] for name in ("head", "query", "slot"))
    split = jax.sharding.Mesh(
        mesh.devices.reshape(heads, halves, slots // 2, 2), ("head", "query", "chip", "core")
    )
    slot = ("chip", "core")
    placed = (
        P("head", "query", None),
        P("head", slot, None),
        P("head", slot, None),
        P("head", slot),
        P("head", "query", None),
        P("head", "query"),
    )
    return jax.shard_map(
        local,
        mesh=split,
        in_specs=placed,
        out_specs=(P("head", slot, None), P("head", slot, None), P("head", slot)),
        check_vma=False,
    )
```

```python
import functools
import math

import jax
import jax.numpy as jnp
from jax import lax
from jax.experimental import pallas as pl
from jax.experimental.pallas import tpu as pltpu
from jax.sharding import PartitionSpec as P

EPS = 1e-06
LOG2E = math.log2(math.e)
F32 = jnp.float32
BF16 = jnp.bfloat16
MIB = 1024 * 1024
STAT = 8
PIECES = 4
ROWS = 256


def whole(shape):
    return pl.BlockSpec(shape, lambda *_: (0,) * len(shape))


def call(kernel, outs, scratch, *args, raw=(), raw_outs=(), cost=None, mib=32, name=None):
    outs = [o if isinstance(o[1], type) else (o, F32) for o in outs]
    anywhere = pl.BlockSpec(memory_space=pl.ANY)
    return pl.pallas_call(
        kernel,
        grid=(1,),
        out_shape=[jax.ShapeDtypeStruct(o, t) for o, t in outs],
        in_specs=[anywhere if i in raw else whole(a.shape) for i, a in enumerate(args)],
        out_specs=[anywhere if i in raw_outs else whole(o) for i, (o, _) in enumerate(outs)],
        scratch_shapes=scratch,
        compiler_params=pltpu.CompilerParams(vmem_limit_bytes=mib * MIB),
        cost_estimate=cost,
        name=name,
    )(*args)


def begin(pairs, sems):
    copies = [pltpu.make_async_copy(a, b, sems.at[i]) for i, (a, b) in enumerate(pairs)]
    for copy in copies:
        copy.start()
    return copies


def contract(a, b, dims):
    return lax.dot_general(a, b, ((dims[:1], dims[1:]), ((), ())), preferred_element_type=F32)


def spread_bias(bias_ref, out_ref):
    slots = bias_ref.shape[1]
    out_ref[...] = jnp.broadcast_to(bias_ref[...] * LOG2E, (128, slots)).T


def tiled_lanes(x, times):
    return jnp.concatenate([x] * times, axis=1)


def forward_kernel(
    scale, q_hbm, k_hbm, v_hbm, bias_ref, out_hbm, q_ref, k_ref, v_ref, out_ref, bias_s, vt_s, sems, out_sems
):
    rows, dim = q_ref.shape
    half = dim // 2
    steps = rows // ROWS
    k_copy, first_copy, v_copy, rest_copy = begin(
        [
            (k_hbm, k_ref),
            (q_hbm.at[pl.ds(0, ROWS)], q_ref.at[pl.ds(0, ROWS)]),
            (v_hbm, v_ref),
            (q_hbm.at[pl.ds(ROWS, rows - ROWS)], q_ref.at[pl.ds(ROWS, rows - ROWS)]),
        ],
        sems,
    )
    spread_bias(bias_ref, bias_s)
    k_copy.wait()
    first_copy.wait()
    out_copies = []
    for r in range(steps):
        if r == 1:
            rest_copy.wait()
        q = q_ref[r * ROWS : (r + 1) * ROWS, :]
        s = contract(k_ref[...], q, (1, 1)) * (scale * LOG2E) + tiled_lanes(bias_s[...], ROWS // 128)
        top = jnp.max(s, axis=0, keepdims=True)
        e = jnp.exp2(s - top)
        total = jnp.sum(e, axis=0, keepdims=True)
        if r == 0:
            v_copy.wait()
            vt_s[...] = v_ref[...].T
        o = contract(vt_s[...], e.astype(BF16), (1, 0))
        for g in range(ROWS // 128):
            block = r * (ROWS // 128) + g
            lanes = slice(g * 128, (g + 1) * 128)
            for c in range(2):
                out_ref[2 * block + c, :half, :] = o[c * half : (c + 1) * half, lanes]
                out_ref[2 * block + c, half : half + 1, :] = top[:, lanes]
                out_ref[2 * block + c, half + 1 : half + 2, :] = total[:, lanes]
                out_ref[2 * block + c, half + 2 :, :] = jnp.zeros((STAT - 2, 128), F32)
        done = pl.ds(r * (ROWS // 64), ROWS // 64)
        copy = pltpu.make_async_copy(out_ref.at[done], out_hbm.at[done], out_sems.at[r])
        copy.start()
        out_copies.append(copy)
    for copy in out_copies:
        copy.wait()


def combine_kernel(got_ref, t_ref, tl_ref, far_ref, out_ref, all_ref, t_s):
    n = got_ref.shape[0]
    half = got_ref.shape[1] - STAT
    core = lax.axis_index("core")
    tops = got_ref[:, half, :]
    totals = got_ref[:, half + 1, :]
    top = jnp.max(tops, axis=0, keepdims=True)
    factor = jnp.exp2(tops - top)
    total = jnp.sum(totals * factor, axis=0, keepdims=True)
    summed = got_ref[0, :half, :] * factor[0:1, :]
    for i in range(1, n):
        summed += got_ref[i, :half, :] * factor[i : i + 1, :]
    outputs = summed / total
    lse2 = top + jnp.log2(total)
    t_s[...] = t_ref[...].T
    start = pl.multiple_of(core * half, half)
    grad_out = outputs - t_s[pl.ds(start, half), :]
    grad_lse = lse2 * math.log(2.0) - tl_ref[pl.ds(lax.axis_index("chip"), 1), :]
    part = jnp.sum(grad_out * outputs, axis=0, keepdims=True)
    first = jnp.where(core == 0, 1.0, 0.0).astype(F32)
    out_ref[:half, :] = grad_out
    out_ref[half : half + 1, :] = lse2
    out_ref[half + 1 : half + 2, :] = part - first * grad_lse
    out_ref[half + 2 :, :] = jnp.zeros((STAT - 2, 128), F32)
    mine = out_ref[...]
    far = far_ref[...]
    for i in range(all_ref.shape[0]):
        all_ref[i, : half + STAT, :] = mine
        all_ref[i, half + STAT :, :] = far


def gather_rows(core, ga_ref, gb_ref, half, grad_s, blocks):
    for b in blocks:
        lanes = slice(b * 128, (b + 1) * 128)
        grad_s[pl.ds(pl.multiple_of(core * half, half), half), lanes] = ga_ref[b, :half, :].astype(BF16)
        grad_s[pl.ds(pl.multiple_of((1 - core) * half, half), half), lanes] = gb_ref[b, :half, :].astype(BF16)


def backward_rows(scale, r, q_ref, ga_ref, gb_ref, k_ref, v_ref, bias_s, grad_s):
    half = k_ref.shape[1] // 2
    blocks = range(r * (ROWS // 128), (r + 1) * (ROWS // 128))
    lse2 = jnp.concatenate([ga_ref[b, half : half + 1, :] for b in blocks], axis=1)
    shift = jnp.concatenate(
        [ga_ref[b, half + 1 : half + 2, :] + gb_ref[b, half + 1 : half + 2, :] for b in blocks], axis=1
    )
    grad_out = grad_s[:, r * ROWS : (r + 1) * ROWS]
    q = q_ref[r * ROWS : (r + 1) * ROWS, :]
    s = contract(k_ref[...], q, (1, 1)) * (scale * LOG2E) + tiled_lanes(bias_s[...], ROWS // 128)
    p = jnp.exp2(s - lse2)
    inner = contract(v_ref[...], grad_out, (1, 0))
    d = p * (inner - shift)
    gv = contract(p.astype(BF16), grad_out, (1, 1))
    gk = contract(d.astype(BF16), q, (1, 0))
    gb = d[:, :128]
    for g in range(1, ROWS // 128):
        gb = gb + d[:, g * 128 : (g + 1) * 128]
    return gk, gv, gb


def near_kernel(
    scale, q_ref, ga_ref, gb_ref, k_ref, v_ref, bias_ref,
    gk_ref, gv_ref, gb_out_ref, far_ref, done_ref, bias_s, grad_s
):
    core = lax.axis_index("core")
    half = k_ref.shape[1] // 2
    spread_bias(bias_ref, bias_s)
    gather_rows(core, ga_ref, gb_ref, half, grad_s, range(ga_ref.shape[0]))
    skip = half + STAT
    for b in range(ga_ref.shape[0]):
        far_ref[pl.ds(pl.multiple_of(b * 128 + core * 64, 64), 64), :] = ga_ref[b, skip:, :].astype(BF16)
        far_ref[pl.ds(pl.multiple_of(b * 128 + (1 - core) * 64, 64), 64), :] = gb_ref[b, skip:, :].astype(BF16)
    done_ref[...] = jnp.zeros(done_ref.shape, F32)
    for r in range(q_ref.shape[0] // ROWS):
        gk, gv, gb = backward_rows(scale, r, q_ref, ga_ref, gb_ref, k_ref, v_ref, bias_s, grad_s)
        if r == 0:
            gk_ref[...], gv_ref[...], gb_out_ref[...] = gk, gv, gb
        else:
            gk_ref[...] += gk
            gv_ref[...] += gv
            gb_out_ref[...] += gb


def far_kernel(
    scale, q_hbm, ga_hbm, gb_hbm, k_hbm, v_hbm, bias_ref, gk0_hbm, gv0_hbm, gb0_hbm, done_ref,
    gk_ref, gv_ref, gb_out_ref, sq_ref, q_ref, ga_ref, gb_ref, k_ref, v_ref, gk0_ref, gv0_ref, gb0_ref, bias_s, grad_s, gb_s, sems
):
    core = lax.axis_index("core")
    half = k_ref.shape[1] // 2
    n = ga_ref.shape[0]
    lead = min(n, ROWS // 128)
    front, back = pl.ds(0, lead), pl.ds(lead, n - lead)
    copies = begin(
        [
            (k_hbm, k_ref),
            (q_hbm.at[pl.ds(0, ROWS)], q_ref.at[pl.ds(0, ROWS)]),
            (ga_hbm.at[front], ga_ref.at[front]),
            (gb_hbm.at[front], gb_ref.at[front]),
            (v_hbm, v_ref),
        ]
        + [
            (q_hbm.at[pl.ds(ROWS, q_ref.shape[0] - ROWS)], q_ref.at[pl.ds(ROWS, q_ref.shape[0] - ROWS)]),
            (ga_hbm.at[back], ga_ref.at[back]),
            (gb_hbm.at[back], gb_ref.at[back]),
        ]
        * (n > lead)
        + [(gk0_hbm, gk0_ref), (gv0_hbm, gv0_ref), (gb0_hbm, gb0_ref)],
        sems,
    )
    spread_bias(bias_ref, bias_s)
    for copy in copies[:5]:
        copy.wait()
    gather_rows(core, ga_ref, gb_ref, half, grad_s, range(lead))
    for r in range(q_ref.shape[0] // ROWS):
        if r == 1:
            for copy in copies[5:-3]:
                copy.wait()
            gather_rows(core, ga_ref, gb_ref, half, grad_s, range(lead, n))
        gk, gv, gb = backward_rows(scale, r, q_ref, ga_ref, gb_ref, k_ref, v_ref, bias_s, grad_s)
        if r == 0:
            gk_ref[...], gv_ref[...], gb_s[...] = gk, gv, gb
        else:
            gk_ref[...] += gk
            gv_ref[...] += gv
            gb_s[...] += gb
    for copy in copies[-3:]:
        copy.wait()
    gk = (gk_ref[...] + gk0_ref[...]) * scale
    gk_ref[...] = gk
    gv = gv_ref[...] + gv0_ref[...]
    gv_ref[...] = gv
    gb = jnp.sum((gb_s[...] + gb0_ref[...]).T, axis=0, keepdims=True)
    gb_out_ref[...] = gb
    lane = lax.broadcasted_iota(jnp.int32, (1, 128), 1)
    sums = [jnp.sum(x * x) for x in (gk, gv, gb)]
    row = jnp.where(lane == 0, sums[0], jnp.where(lane == 1, sums[1], sums[2]))
    sq_ref[...] = jnp.broadcast_to(row, sq_ref.shape)


def scale_kernel(counts, sq_ref, gk_hbm, gv_hbm, gb_ref, ok_hbm, ov_hbm, ob_ref, gk_ref, gv_ref, sems, out_sems):
    rows = gk_ref.shape[0]
    size = rows // PIECES
    spans = [pl.ds(i * size, size) for i in range(PIECES)]
    pairs = [(hbm.at[span], ref.at[span]) for hbm, ref in ((gk_hbm, gk_ref), (gv_hbm, gv_ref)) for span in spans]
    copies = begin(pairs, sems)
    total = jnp.sum(sq_ref[...], axis=0, keepdims=True)
    lane = lax.broadcasted_iota(jnp.int32, (1, 128), 1)
    factors = []
    for i, count in enumerate(counts):
        mean = jnp.sum(jnp.where(lane == i, total, 0.0), axis=1, keepdims=True) / count
        factors.append(1.0 / jnp.sqrt(mean + EPS))
    ob_ref[...] = gb_ref[...] * factors[2]
    outs = []
    for i, (ref, out) in enumerate(((gk_ref, ok_hbm), (gv_ref, ov_hbm))):
        for j, span in enumerate(spans):
            copies[i * PIECES + j].wait()
            ref[span, :] = ref[span, :] * factors[i]
            copy = pltpu.make_async_copy(ref.at[span], out.at[span], out_sems.at[i * PIECES + j])
            copy.start()
            outs.append(copy)
    for copy in outs:
        copy.wait()


def local(queries, keys, values, bias, targets, target_lse):
    q, k, v, t = queries[0], keys[0], values[0], targets[0]
    rows, dim = q.shape
    slots = k.shape[0]
    half = dim // 2
    scale = dim ** (-0.5)
    n_chip = lax.axis_size("chip")
    n_slot = 2 * n_chip
    n_all = lax.axis_size("head") * n_slot
    chip, core = lax.axis_index("chip"), lax.axis_index("core")
    dma = pltpu.SemaphoreType.DMA
    across = [(0, 1), (1, 0)]
    wide = pltpu.VMEM((slots, 128), F32)

    (parts,) = call(
        functools.partial(forward_kernel, scale),
        [(n_slot, half + STAT, 128)],
        [
            pltpu.VMEM((rows, dim), BF16), pltpu.VMEM((slots, dim), BF16), pltpu.VMEM((slots, dim), BF16),
            pltpu.VMEM((n_slot, half + STAT, 128), F32), wide, pltpu.VMEM((dim, slots), BF16),
            dma((4,)), dma((rows // ROWS,)),
        ],
        q, k, v, bias, raw=(0, 1, 2), raw_outs=(0,), mib=62, name="forward",
    )
    parts, q_later = lax.optimization_barrier((parts, q))
    got = lax.all_to_all(parts, ("chip", "core"), 0, 0)
    own = lax.dynamic_slice_in_dim(q_later, (chip * 2 + core) * 64, 64, 0).astype(F32)
    far = lax.ppermute(own, "query", across)
    t_own = lax.dynamic_slice_in_dim(t, chip * 128, 128, 0)
    mine, spread = call(
        combine_kernel,
        [(half + STAT, 128), (n_chip, half + STAT + 64, 128)],
        [pltpu.VMEM((dim, 128), F32)],
        got, t_own, target_lse.reshape(rows // 128, 128), far, name="combine",
    )

    def trade(x):
        return lax.all_to_all(x, "chip", 0, 0)

    near_a = trade(spread)
    theirs = lax.ppermute(mine, "query", across)
    near_a, theirs = lax.optimization_barrier((near_a, theirs))
    near_b = lax.ppermute(near_a, "core", across)
    far_a = trade(jnp.broadcast_to(theirs[None], (n_chip,) + theirs.shape))
    cost = pl.CostEstimate(flops=8 * rows * slots * dim, bytes_accessed=4 << 20, transcendentals=rows * slots)
    grad_s = pltpu.VMEM((dim, rows), BF16)
    mat = (slots, dim)
    held = pltpu.VMEM((n_chip, half + STAT, 128), F32)
    gk, gv, gb, q_far, done = call(
        functools.partial(near_kernel, scale),
        [mat, mat, (slots, 128), ((rows, dim), BF16), (8, 128)],
        [wide, grad_s],
        q, near_a, near_b, k, v, bias, cost=cost, mib=62, name="backward_near",
    )
    far_a, done = lax.optimization_barrier((far_a, done))
    far_b = lax.ppermute(far_a, "core", across)
    gk, gv, gb, sq = call(
        functools.partial(far_kernel, scale),
        [mat, mat, (1, slots), (n_chip, 128)],
        [
            pltpu.VMEM((rows, dim), BF16), held, held, pltpu.VMEM((slots, dim), BF16), pltpu.VMEM((slots, dim), BF16),
            pltpu.VMEM(mat, F32), pltpu.VMEM(mat, F32), wide, wide, grad_s, wide, dma((11,)),
        ],
        q_far, far_a, far_b, k, v, bias, gk, gv, gb, done, raw=(0, 1, 2, 3, 4, 6, 7, 8), cost=cost, mib=62, name="backward_far",
    )
    plane = jnp.sum(lax.all_to_all(sq.reshape(n_chip, 1, 128), "chip", 0, 0), axis=0)
    n_line = 2 * lax.axis_size("head")
    line = jnp.broadcast_to(plane[None], (n_line, 1, 128))
    sq_all = lax.all_to_all(line, ("head", "core"), 0, 0)
    counts = (float(n_all * slots * dim), float(n_all * slots * dim), float(n_all * slots))
    ok, ov, ob = call(
        functools.partial(scale_kernel, counts),
        [mat, mat, (1, slots)],
        [pltpu.VMEM(mat, F32), pltpu.VMEM(mat, F32), dma((2 * PIECES,)), dma((2 * PIECES,))],
        sq_all.reshape(n_line, 128), gk, gv, gb, raw=(1, 2), raw_outs=(0, 1), mib=62, name="normalize",
    )
    return ok[None], ov[None], ob


def solution(mesh):
    heads, halves, slots = (mesh.shape[name] for name in ("head", "query", "slot"))
    split = jax.sharding.Mesh(
        mesh.devices.reshape(heads, halves, slots // 2, 2), ("head", "query", "chip", "core")
    )
    slot = ("chip", "core")
    placed = (
        P("head", "query", None),
        P("head", slot, None),
        P("head", slot, None),
        P("head", slot),
        P("head", "query", None),
        P("head", "query"),
    )
    return jax.shard_map(
        local,
        mesh=split,
        in_specs=placed,
        out_specs=(P("head", slot, None), P("head", slot, None), P("head", slot)),
        check_vma=False,
    )
```

```python
import functools
import math

import jax
import jax.numpy as jnp
from jax import lax
from jax.experimental import pallas as pl
from jax.experimental.pallas import tpu as pltpu
from jax.sharding import PartitionSpec as P

EPS = 1e-06
LOG2E = math.log2(math.e)
F32 = jnp.float32
BF16 = jnp.bfloat16
MIB = 1024 * 1024
STAT = 8
PIECES = 4
ROWS = 256


def whole(shape):
    return pl.BlockSpec(shape, lambda *_: (0,) * len(shape))


def call(kernel, outs, scratch, *args, raw=(), raw_outs=(), cost=None, mib=32, name=None, placed=True):
    outs = [o if isinstance(o[1], type) else (o, F32) for o in outs]
    anywhere = pl.BlockSpec(memory_space=pltpu.HBM)
    held = pl.BlockSpec(memory_space=pltpu.VMEM)
    return pl.pallas_call(
        kernel,
        grid=() if placed else (1,),
        out_shape=[jax.ShapeDtypeStruct(o, t) for o, t in outs],
        in_specs=[anywhere if i in raw else held if placed else whole(a.shape) for i, a in enumerate(args)],
        out_specs=[anywhere if i in raw_outs else held if placed else whole(o) for i, (o, _) in enumerate(outs)],
        scratch_shapes=scratch,
        compiler_params=pltpu.CompilerParams(vmem_limit_bytes=mib * MIB),
        cost_estimate=cost,
        name=name,
    )(*args)


def begin(pairs, sems):
    copies = [pltpu.make_async_copy(a, b, sems.at[i]) for i, (a, b) in enumerate(pairs)]
    for copy in copies:
        copy.start()
    return copies


def contract(a, b, dims):
    return lax.dot_general(a, b, ((dims[:1], dims[1:]), ((), ())), preferred_element_type=F32)


def spread_bias(bias_ref, out_ref):
    slots = bias_ref.shape[1]
    out_ref[...] = jnp.broadcast_to(bias_ref[...] * LOG2E, (128, slots)).T


def tiled_lanes(x, times):
    return jnp.concatenate([x] * times, axis=1)


def forward_kernel(
    scale, q_hbm, k_hbm, v_hbm, bias_ref, out_hbm, own_ref, q_ref, k_ref, v_ref, out_ref, bias_s, vt_s, sems, out_sems
):
    rows, dim = q_ref.shape
    half = dim // 2
    steps = rows // ROWS
    k_copy, first_copy, v_copy, rest_copy = begin(
        [
            (k_hbm, k_ref),
            (q_hbm.at[pl.ds(0, ROWS)], q_ref.at[pl.ds(0, ROWS)]),
            (v_hbm, v_ref),
            (q_hbm.at[pl.ds(ROWS, rows - ROWS)], q_ref.at[pl.ds(ROWS, rows - ROWS)]),
        ],
        sems,
    )
    spread_bias(bias_ref, bias_s)
    k_copy.wait()
    first_copy.wait()
    out_copies = []
    for r in range(steps):
        if r == 1:
            rest_copy.wait()
        q = q_ref[r * ROWS : (r + 1) * ROWS, :]
        s = contract(k_ref[...], q, (1, 1)) * (scale * LOG2E) + tiled_lanes(bias_s[...], ROWS // 128)
        top = jnp.max(s, axis=0, keepdims=True)
        e = jnp.exp2(s - top)
        total = jnp.sum(e, axis=0, keepdims=True)
        if r == 0:
            v_copy.wait()
            vt_s[...] = v_ref[...].T
        o = contract(vt_s[...], e.astype(BF16), (1, 0))
        for g in range(ROWS // 128):
            block = r * (ROWS // 128) + g
            lanes = slice(g * 128, (g + 1) * 128)
            for c in range(2):
                out_ref[2 * block + c, :half, :] = o[c * half : (c + 1) * half, lanes]
                out_ref[2 * block + c, half : half + 1, :] = top[:, lanes]
                out_ref[2 * block + c, half + 1 : half + 2, :] = total[:, lanes]
                out_ref[2 * block + c, half + 2 :, :] = jnp.zeros((STAT - 2, 128), F32)
        done = pl.ds(r * (ROWS // 64), ROWS // 64)
        copy = pltpu.make_async_copy(out_ref.at[done], out_hbm.at[done], out_sems.at[r])
        copy.start()
        out_copies.append(copy)
    first = (lax.axis_index("chip") * 2 + lax.axis_index("core")) * 64
    own_ref[...] = q_ref[pl.ds(pl.multiple_of(first, 64), 64), :].astype(F32)
    for copy in out_copies:
        copy.wait()


def combine_kernel(got_ref, t_ref, tl_ref, far_ref, out_ref, all_ref, t_s):
    n = got_ref.shape[0]
    half = got_ref.shape[1] - STAT
    core = lax.axis_index("core")
    tops = got_ref[:, half, :]
    totals = got_ref[:, half + 1, :]
    top = jnp.max(tops, axis=0, keepdims=True)
    factor = jnp.exp2(tops - top)
    total = jnp.sum(totals * factor, axis=0, keepdims=True)
    summed = got_ref[0, :half, :] * factor[0:1, :]
    for i in range(1, n):
        summed += got_ref[i, :half, :] * factor[i : i + 1, :]
    outputs = summed / total
    lse2 = top + jnp.log2(total)
    t_s[...] = t_ref[...].T
    start = pl.multiple_of(core * half, half)
    grad_out = outputs - t_s[pl.ds(start, half), :]
    grad_lse = lse2 * math.log(2.0) - tl_ref[pl.ds(lax.axis_index("chip"), 1), :]
    part = jnp.sum(grad_out * outputs, axis=0, keepdims=True)
    first = jnp.where(core == 0, 1.0, 0.0).astype(F32)
    out_ref[:half, :] = grad_out
    out_ref[half : half + 1, :] = lse2
    out_ref[half + 1 : half + 2, :] = part - first * grad_lse
    out_ref[half + 2 :, :] = jnp.zeros((STAT - 2, 128), F32)
    mine = out_ref[...]
    far = far_ref[...]
    for i in range(all_ref.shape[0]):
        all_ref[i, : half + STAT, :] = mine
        all_ref[i, half + STAT :, :] = far


def gather_rows(core, ga_ref, gb_ref, half, grad_s, blocks):
    for b in blocks:
        lanes = slice(b * 128, (b + 1) * 128)
        grad_s[pl.ds(pl.multiple_of(core * half, half), half), lanes] = ga_ref[b, :half, :].astype(BF16)
        grad_s[pl.ds(pl.multiple_of((1 - core) * half, half), half), lanes] = gb_ref[b, :half, :].astype(BF16)


def backward_rows(scale, r, q_ref, ga_ref, gb_ref, k_ref, v_ref, bias_s, grad_s):
    half = k_ref.shape[1] // 2
    blocks = range(r * (ROWS // 128), (r + 1) * (ROWS // 128))
    lse2 = jnp.concatenate([ga_ref[b, half : half + 1, :] for b in blocks], axis=1)
    shift = jnp.concatenate(
        [ga_ref[b, half + 1 : half + 2, :] + gb_ref[b, half + 1 : half + 2, :] for b in blocks], axis=1
    )
    grad_out = grad_s[:, r * ROWS : (r + 1) * ROWS]
    q = q_ref[r * ROWS : (r + 1) * ROWS, :]
    s = contract(k_ref[...], q, (1, 1)) * (scale * LOG2E) + tiled_lanes(bias_s[...], ROWS // 128)
    p = jnp.exp2(s - lse2)
    inner = contract(v_ref[...], grad_out, (1, 0))
    d = p * (inner - shift)
    gv = contract(p.astype(BF16), grad_out, (1, 1))
    gk = contract(d.astype(BF16), q, (1, 0))
    gb = d[:, :128]
    for g in range(1, ROWS // 128):
        gb = gb + d[:, g * 128 : (g + 1) * 128]
    return gk, gv, gb


def near_kernel(
    scale, q_ref, ga_ref, gb_ref, k_ref, v_ref, bias_ref,
    gk_ref, gv_ref, gb_out_ref, far_ref, done_ref, bias_s, grad_s
):
    core = lax.axis_index("core")
    half = k_ref.shape[1] // 2
    spread_bias(bias_ref, bias_s)
    gather_rows(core, ga_ref, gb_ref, half, grad_s, range(ga_ref.shape[0]))
    skip = half + STAT
    for b in range(ga_ref.shape[0]):
        far_ref[pl.ds(pl.multiple_of(b * 128 + core * 64, 64), 64), :] = ga_ref[b, skip:, :].astype(BF16)
        far_ref[pl.ds(pl.multiple_of(b * 128 + (1 - core) * 64, 64), 64), :] = gb_ref[b, skip:, :].astype(BF16)
    done_ref[...] = jnp.zeros(done_ref.shape, F32)
    for r in range(q_ref.shape[0] // ROWS):
        gk, gv, gb = backward_rows(scale, r, q_ref, ga_ref, gb_ref, k_ref, v_ref, bias_s, grad_s)
        if r == 0:
            gk_ref[...], gv_ref[...], gb_out_ref[...] = gk, gv, gb
        else:
            gk_ref[...] += gk
            gv_ref[...] += gv
            gb_out_ref[...] += gb


def far_kernel(
    scale, q_hbm, ga_ref, gb_ref, k_hbm, v_hbm, bias_ref, gk0_hbm, gv0_hbm, gb0_hbm, done_ref,
    gk_ref, gv_ref, gb_out_ref, sq_ref, q_ref, k_ref, v_ref, gk0_ref, gv0_ref, gb0_ref, bias_s, grad_s, gb_s, sems
):
    core = lax.axis_index("core")
    half = k_ref.shape[1] // 2
    rows = q_ref.shape[0]
    front, back = pl.ds(0, ROWS), pl.ds(ROWS, rows - ROWS)
    copies = begin(
        [
            (k_hbm, k_ref),
            (q_hbm.at[front], q_ref.at[front]),
            (v_hbm, v_ref),
            (q_hbm.at[back], q_ref.at[back]),
            (gk0_hbm, gk0_ref),
            (gv0_hbm, gv0_ref),
            (gb0_hbm, gb0_ref),
        ],
        sems,
    )
    spread_bias(bias_ref, bias_s)
    gather_rows(core, ga_ref, gb_ref, half, grad_s, range(ga_ref.shape[0]))
    for copy in copies[:3]:
        copy.wait()
    for r in range(rows // ROWS):
        if r == 1:
            copies[3].wait()
        gk, gv, gb = backward_rows(scale, r, q_ref, ga_ref, gb_ref, k_ref, v_ref, bias_s, grad_s)
        if r == 0:
            gk_ref[...], gv_ref[...], gb_s[...] = gk, gv, gb
        else:
            gk_ref[...] += gk
            gv_ref[...] += gv
            gb_s[...] += gb
    for copy in copies[-3:]:
        copy.wait()
    gk = (gk_ref[...] + gk0_ref[...]) * scale
    gk_ref[...] = gk
    gv = gv_ref[...] + gv0_ref[...]
    gv_ref[...] = gv
    gb = jnp.sum((gb_s[...] + gb0_ref[...]).T, axis=0, keepdims=True)
    gb_out_ref[...] = gb
    lane = lax.broadcasted_iota(jnp.int32, (1, 128), 1)
    sums = [jnp.sum(x * x) for x in (gk, gv, gb)]
    row = jnp.where(lane == 0, sums[0], jnp.where(lane == 1, sums[1], sums[2]))
    sq_ref[...] = jnp.broadcast_to(row, sq_ref.shape)


def scale_kernel(counts, sq_ref, gk_ref, gv_ref, gb_ref, ok_hbm, ov_hbm, ob_ref, sk_ref, sv_ref, sems):
    size = gk_ref.shape[0] // PIECES
    total = jnp.sum(sq_ref[...], axis=0, keepdims=True)
    lane = lax.broadcasted_iota(jnp.int32, (1, 128), 1)
    factors = []
    for i, count in enumerate(counts):
        mean = jnp.sum(jnp.where(lane == i, total, 0.0), axis=1, keepdims=True) / count
        factors.append(1.0 / jnp.sqrt(mean + EPS))
    copies = []
    for i, (g_ref, s_ref, out) in enumerate(((gk_ref, sk_ref, ok_hbm), (gv_ref, sv_ref, ov_hbm))):
        for j in range(PIECES):
            span = pl.ds(j * size, size)
            s_ref[span, :] = g_ref[span, :] * factors[i]
            copy = pltpu.make_async_copy(s_ref.at[span], out.at[span], sems.at[i * PIECES + j])
            copy.start()
            copies.append(copy)
    ob_ref[...] = gb_ref[...] * factors[2]
    for copy in copies:
        copy.wait()


def local(queries, keys, values, bias, targets, target_lse):
    q, k, v, t = queries[0], keys[0], values[0], targets[0]
    rows, dim = q.shape
    slots = k.shape[0]
    half = dim // 2
    scale = dim ** (-0.5)
    n_chip = lax.axis_size("chip")
    n_slot = 2 * n_chip
    n_all = lax.axis_size("head") * n_slot
    chip, core = lax.axis_index("chip"), lax.axis_index("core")
    dma = pltpu.SemaphoreType.DMA
    across = [(0, 1), (1, 0)]
    wide = pltpu.VMEM((slots, 128), F32)

    parts, own = call(
        functools.partial(forward_kernel, scale),
        [(n_slot, half + STAT, 128), (64, dim)],
        [
            pltpu.VMEM((rows, dim), BF16), pltpu.VMEM((slots, dim), BF16), pltpu.VMEM((slots, dim), BF16),
            pltpu.VMEM((n_slot, half + STAT, 128), F32), wide, pltpu.VMEM((dim, slots), BF16),
            dma((4,)), dma((rows // ROWS,)),
        ],
        q, k, v, bias, raw=(0, 1, 2), raw_outs=(0,), mib=62, name="forward",
    )
    got = lax.all_to_all(parts, ("chip", "core"), 0, 0)
    far = lax.ppermute(own, "query", across)
    t_own = lax.dynamic_slice_in_dim(t, chip * 128, 128, 0)
    mine, spread = call(
        combine_kernel,
        [(half + STAT, 128), (n_chip, half + STAT + 64, 128)],
        [pltpu.VMEM((dim, 128), F32)],
        got, t_own, target_lse.reshape(rows // 128, 128), far, name="combine",
    )

    def trade(x):
        return lax.all_to_all(x, "chip", 0, 0)

    near_a = trade(spread)
    theirs = lax.ppermute(mine, "query", across)
    theirs_all = jnp.broadcast_to(theirs[None], (n_chip,) + theirs.shape)
    near_a, theirs_all = lax.optimization_barrier((near_a, theirs_all))
    near_b = lax.ppermute(near_a, "core", across)
    far_a = trade(theirs_all)
    cost = pl.CostEstimate(flops=8 * rows * slots * dim, bytes_accessed=4 << 20, transcendentals=rows * slots)
    grad_s = pltpu.VMEM((dim, rows), BF16)
    mat = (slots, dim)
    gk, gv, gb, q_far, done = call(
        functools.partial(near_kernel, scale),
        [mat, mat, (slots, 128), ((rows, dim), BF16), (8, 128)],
        [wide, grad_s],
        q, near_a, near_b, k, v, bias, placed=False, cost=cost, mib=52, name="backward_near",
    )
    far_a, done = lax.optimization_barrier((far_a, done))
    far_b = lax.ppermute(far_a, "core", across)
    gk, gv, gb, sq = call(
        functools.partial(far_kernel, scale),
        [mat, mat, (1, slots), (n_chip, 128)],
        [
            pltpu.VMEM((rows, dim), BF16), pltpu.VMEM((slots, dim), BF16), pltpu.VMEM((slots, dim), BF16),
            pltpu.VMEM(mat, F32), pltpu.VMEM(mat, F32), wide, wide, grad_s, wide, dma((7,)),
        ],
        q_far, far_a, far_b, k, v, bias, gk, gv, gb, done, raw=(0, 3, 4, 6, 7, 8), cost=cost, mib=52, name="backward_far",
    )
    plane = jnp.sum(lax.all_to_all(sq.reshape(n_chip, 1, 128), "chip", 0, 0), axis=0)
    n_line = 2 * lax.axis_size("head")
    line = jnp.broadcast_to(plane[None], (n_line, 1, 128))
    sq_all = lax.all_to_all(line, ("head", "core"), 0, 0)
    counts = (float(n_all * slots * dim), float(n_all * slots * dim), float(n_all * slots))
    ok, ov, ob = call(
        functools.partial(scale_kernel, counts),
        [mat, mat, (1, slots)],
        [pltpu.VMEM(mat, F32), pltpu.VMEM(mat, F32), dma((2 * PIECES,))],
        sq_all.reshape(n_line, 128), gk, gv, gb, raw_outs=(0, 1), mib=32, name="normalize",
    )
    return ok[None], ov[None], ob


def solution(mesh):
    heads, halves, slots = (mesh.shape[name] for name in ("head", "query", "slot"))
    split = jax.sharding.Mesh(
        mesh.devices.reshape(heads, halves, slots // 2, 2), ("head", "query", "chip", "core")
    )
    slot = ("chip", "core")
    placed = (
        P("head", "query", None),
        P("head", slot, None),
        P("head", slot, None),
        P("head", slot),
        P("head", "query", None),
        P("head", "query"),
    )
    return jax.shard_map(
        local,
        mesh=split,
        in_specs=placed,
        out_specs=(P("head", slot, None), P("head", slot, None), P("head", slot)),
        check_vma=False,
    )
```

```python
import functools
import math

import jax
import jax.numpy as jnp
from jax import lax
from jax.experimental import pallas as pl
from jax.experimental.pallas import tpu as pltpu
from jax.sharding import PartitionSpec as P

EPS = 1e-06
LOG2E = math.log2(math.e)
F32 = jnp.float32
BF16 = jnp.bfloat16
MIB = 1024 * 1024
STAT = 8
PIECES = 4
SLOTS = 512
ROWS = 256


def whole(shape):
    return pl.BlockSpec(shape, lambda *_: (0,) * len(shape))


def call(kernel, outs, scratch, *args, raw=(), raw_outs=(), cost=None, mib=32, name=None, placed=True):
    outs = [o if isinstance(o[1], type) else (o, F32) for o in outs]
    anywhere = pl.BlockSpec(memory_space=pltpu.HBM)
    held = pl.BlockSpec(memory_space=pltpu.VMEM)
    return pl.pallas_call(
        kernel,
        grid=() if placed else (1,),
        out_shape=[jax.ShapeDtypeStruct(o, t) for o, t in outs],
        in_specs=[anywhere if i in raw else held if placed else whole(a.shape) for i, a in enumerate(args)],
        out_specs=[anywhere if i in raw_outs else held if placed else whole(o) for i, (o, _) in enumerate(outs)],
        scratch_shapes=scratch,
        compiler_params=pltpu.CompilerParams(vmem_limit_bytes=mib * MIB),
        cost_estimate=cost,
        name=name,
    )(*args)


def begin(pairs, sems):
    copies = [pltpu.make_async_copy(a, b, sems.at[i]) for i, (a, b) in enumerate(pairs)]
    for copy in copies:
        copy.start()
    return copies


def contract(a, b, dims):
    return lax.dot_general(a, b, ((dims[:1], dims[1:]), ((), ())), preferred_element_type=F32)


def spread_bias(bias_ref, out_ref):
    slots = bias_ref.shape[1]
    out_ref[...] = jnp.broadcast_to(bias_ref[...] * LOG2E, (128, slots)).T


def tiled_lanes(x, times):
    return jnp.concatenate([x] * times, axis=1)


def forward_piece(scale, q, k, vt, bias):
    s = contract(k, q, (1, 1)) * (scale * LOG2E) + bias
    top = jnp.max(s, axis=0, keepdims=True)
    e = jnp.exp2(s - top)
    total = jnp.sum(e, axis=0, keepdims=True)
    return top, total, contract(vt, e.astype(BF16), (1, 0))


def forward_kernel(
    scale, q_hbm, k_hbm, v_hbm, bias_ref, out_hbm, own_ref, q_ref, k_ref, v_ref, out_ref, bias_s, vt_s, sems, out_sems
):
    rows, dim = q_ref.shape
    slots = k_ref.shape[0]
    half = dim // 2
    size = min(SLOTS, slots)
    spans = [slice(i * size, (i + 1) * size) for i in range(slots // size)]
    k_copy, first_copy, v_copy, rest_copy = begin(
        [
            (k_hbm, k_ref),
            (q_hbm.at[pl.ds(0, 128)], q_ref.at[pl.ds(0, 128)]),
            (v_hbm, v_ref),
            (q_hbm.at[pl.ds(128, rows - 128)], q_ref.at[pl.ds(128, rows - 128)]),
        ],
        sems,
    )
    spread_bias(bias_ref, bias_s)
    for copy in (k_copy, first_copy, v_copy):
        copy.wait()
    vt_s[...] = v_ref[...].T
    rest_copy.wait()
    out_copies = []
    for b in range(rows // 128):
        q = q_ref[b * 128 : (b + 1) * 128, :]
        pieces = [forward_piece(scale, q, k_ref[x, :], vt_s[:, x], bias_s[x, :]) for x in spans]
        top = functools.reduce(jnp.maximum, [piece[0] for piece in pieces])
        factors = [jnp.exp2(piece[0] - top) for piece in pieces]
        total = sum(piece[1] * f for piece, f in zip(pieces, factors))
        o = sum(piece[2] * f for piece, f in zip(pieces, factors))
        for c in range(2):
            out_ref[2 * b + c, :half, :] = o[c * half : (c + 1) * half, :]
            out_ref[2 * b + c, half : half + 1, :] = top
            out_ref[2 * b + c, half + 1 : half + 2, :] = total
            out_ref[2 * b + c, half + 2 :, :] = jnp.zeros((STAT - 2, 128), F32)
        done = pl.ds(2 * b, 2)
        copy = pltpu.make_async_copy(out_ref.at[done], out_hbm.at[done], out_sems.at[b])
        copy.start()
        out_copies.append(copy)
    first = (lax.axis_index("chip") * 2 + lax.axis_index("core")) * 64
    own_ref[...] = q_ref[pl.ds(pl.multiple_of(first, 64), 64), :].astype(F32)
    for copy in out_copies:
        copy.wait()


def combine_kernel(got_ref, t_ref, tl_ref, far_ref, out_ref, all_ref, t_s):
    n = got_ref.shape[0]
    half = got_ref.shape[1] - STAT
    core = lax.axis_index("core")
    tops = got_ref[:, half, :]
    totals = got_ref[:, half + 1, :]
    top = jnp.max(tops, axis=0, keepdims=True)
    factor = jnp.exp2(tops - top)
    total = jnp.sum(totals * factor, axis=0, keepdims=True)
    summed = got_ref[0, :half, :] * factor[0:1, :]
    for i in range(1, n):
        summed += got_ref[i, :half, :] * factor[i : i + 1, :]
    outputs = summed / total
    lse2 = top + jnp.log2(total)
    t_s[...] = t_ref[...].T
    start = pl.multiple_of(core * half, half)
    grad_out = outputs - t_s[pl.ds(start, half), :]
    grad_lse = lse2 * math.log(2.0) - tl_ref[pl.ds(lax.axis_index("chip"), 1), :]
    part = jnp.sum(grad_out * outputs, axis=0, keepdims=True)
    first = jnp.where(core == 0, 1.0, 0.0).astype(F32)
    out_ref[:half, :] = grad_out
    out_ref[half : half + 1, :] = lse2
    out_ref[half + 1 : half + 2, :] = part - first * grad_lse
    out_ref[half + 2 :, :] = jnp.zeros((STAT - 2, 128), F32)
    mine = out_ref[...]
    far = far_ref[...]
    for i in range(all_ref.shape[0]):
        all_ref[i, : half + STAT, :] = mine
        all_ref[i, half + STAT :, :] = far


def gather_rows(core, ga_ref, gb_ref, half, grad_s, blocks):
    for b in blocks:
        lanes = slice(b * 128, (b + 1) * 128)
        grad_s[pl.ds(pl.multiple_of(core * half, half), half), lanes] = ga_ref[b, :half, :].astype(BF16)
        grad_s[pl.ds(pl.multiple_of((1 - core) * half, half), half), lanes] = gb_ref[b, :half, :].astype(BF16)


def backward_rows(scale, r, q_ref, ga_ref, gb_ref, k_ref, v_ref, bias_s, grad_s):
    half = k_ref.shape[1] // 2
    blocks = range(r * (ROWS // 128), (r + 1) * (ROWS // 128))
    lse2 = jnp.concatenate([ga_ref[b, half : half + 1, :] for b in blocks], axis=1)
    shift = jnp.concatenate(
        [ga_ref[b, half + 1 : half + 2, :] + gb_ref[b, half + 1 : half + 2, :] for b in blocks], axis=1
    )
    grad_out = grad_s[:, r * ROWS : (r + 1) * ROWS]
    q = q_ref[r * ROWS : (r + 1) * ROWS, :]
    s = contract(k_ref[...], q, (1, 1)) * (scale * LOG2E) + tiled_lanes(bias_s[...], ROWS // 128)
    p = jnp.exp2(s - lse2)
    inner = contract(v_ref[...], grad_out, (1, 0))
    d = p * (inner - shift)
    gv = contract(p.astype(BF16), grad_out, (1, 1))
    gk = contract(d.astype(BF16), q, (1, 0))
    gb = d[:, :128]
    for g in range(1, ROWS // 128):
        gb = gb + d[:, g * 128 : (g + 1) * 128]
    return gk, gv, gb


def near_kernel(
    scale, q_ref, ga_ref, gb_ref, k_ref, v_ref, bias_ref,
    gk_ref, gv_ref, gb_out_ref, far_ref, done_ref, bias_s, grad_s
):
    core = lax.axis_index("core")
    half = k_ref.shape[1] // 2
    spread_bias(bias_ref, bias_s)
    gather_rows(core, ga_ref, gb_ref, half, grad_s, range(ga_ref.shape[0]))
    skip = half + STAT
    for b in range(ga_ref.shape[0]):
        far_ref[pl.ds(pl.multiple_of(b * 128 + core * 64, 64), 64), :] = ga_ref[b, skip:, :].astype(BF16)
        far_ref[pl.ds(pl.multiple_of(b * 128 + (1 - core) * 64, 64), 64), :] = gb_ref[b, skip:, :].astype(BF16)
    done_ref[...] = jnp.zeros(done_ref.shape, F32)
    for r in range(q_ref.shape[0] // ROWS):
        gk, gv, gb = backward_rows(scale, r, q_ref, ga_ref, gb_ref, k_ref, v_ref, bias_s, grad_s)
        if r == 0:
            gk_ref[...], gv_ref[...], gb_out_ref[...] = gk, gv, gb
        else:
            gk_ref[...] += gk
            gv_ref[...] += gv
            gb_out_ref[...] += gb


def far_kernel(
    scale, q_hbm, ga_ref, gb_ref, k_hbm, v_hbm, bias_ref, gk0_hbm, gv0_hbm, gb0_hbm, done_ref,
    gk_ref, gv_ref, gb_out_ref, sq_ref, q_ref, k_ref, v_ref, gk0_ref, gv0_ref, gb0_ref, bias_s, grad_s, gb_s, sems
):
    core = lax.axis_index("core")
    half = k_ref.shape[1] // 2
    rows = q_ref.shape[0]
    front, back = pl.ds(0, ROWS), pl.ds(ROWS, rows - ROWS)
    copies = begin(
        [
            (k_hbm, k_ref),
            (q_hbm.at[front], q_ref.at[front]),
            (v_hbm, v_ref),
            (q_hbm.at[back], q_ref.at[back]),
            (gk0_hbm, gk0_ref),
            (gv0_hbm, gv0_ref),
            (gb0_hbm, gb0_ref),
        ],
        sems,
    )
    spread_bias(bias_ref, bias_s)
    gather_rows(core, ga_ref, gb_ref, half, grad_s, range(ga_ref.shape[0]))
    for copy in copies[:3]:
        copy.wait()
    for r in range(rows // ROWS):
        if r == 1:
            copies[3].wait()
        gk, gv, gb = backward_rows(scale, r, q_ref, ga_ref, gb_ref, k_ref, v_ref, bias_s, grad_s)
        if r == 0:
            gk_ref[...], gv_ref[...], gb_s[...] = gk, gv, gb
        else:
            gk_ref[...] += gk
            gv_ref[...] += gv
            gb_s[...] += gb
    for copy in copies[-3:]:
        copy.wait()
    gk = (gk_ref[...] + gk0_ref[...]) * scale
    gk_ref[...] = gk
    gv = gv_ref[...] + gv0_ref[...]
    gv_ref[...] = gv
    gb = jnp.sum((gb_s[...] + gb0_ref[...]).T, axis=0, keepdims=True)
    gb_out_ref[...] = gb
    lane = lax.broadcasted_iota(jnp.int32, (1, 128), 1)
    sums = [jnp.sum(x * x) for x in (gk, gv, gb)]
    row = jnp.where(lane == 0, sums[0], jnp.where(lane == 1, sums[1], sums[2]))
    sq_ref[...] = jnp.broadcast_to(row, sq_ref.shape)


def scale_kernel(counts, sq_ref, gk_ref, gv_ref, gb_ref, ok_hbm, ov_hbm, ob_ref, sk_ref, sv_ref, sems):
    size = gk_ref.shape[0] // PIECES
    total = jnp.sum(sq_ref[...], axis=0, keepdims=True)
    lane = lax.broadcasted_iota(jnp.int32, (1, 128), 1)
    factors = []
    for i, count in enumerate(counts):
        mean = jnp.sum(jnp.where(lane == i, total, 0.0), axis=1, keepdims=True) / count
        factors.append(1.0 / jnp.sqrt(mean + EPS))
    copies = []
    for i, (g_ref, s_ref, out) in enumerate(((gk_ref, sk_ref, ok_hbm), (gv_ref, sv_ref, ov_hbm))):
        for j in range(PIECES):
            span = pl.ds(j * size, size)
            s_ref[span, :] = g_ref[span, :] * factors[i]
            copy = pltpu.make_async_copy(s_ref.at[span], out.at[span], sems.at[i * PIECES + j])
            copy.start()
            copies.append(copy)
    ob_ref[...] = gb_ref[...] * factors[2]
    for copy in copies:
        copy.wait()


def local(queries, keys, values, bias, targets, target_lse):
    q, k, v, t = queries[0], keys[0], values[0], targets[0]
    rows, dim = q.shape
    slots = k.shape[0]
    half = dim // 2
    scale = dim ** (-0.5)
    n_chip = lax.axis_size("chip")
    n_slot = 2 * n_chip
    n_all = lax.axis_size("head") * n_slot
    chip, core = lax.axis_index("chip"), lax.axis_index("core")
    dma = pltpu.SemaphoreType.DMA
    across = [(0, 1), (1, 0)]
    wide = pltpu.VMEM((slots, 128), F32)

    parts, own = call(
        functools.partial(forward_kernel, scale),
        [(n_slot, half + STAT, 128), (64, dim)],
        [
            pltpu.VMEM((rows, dim), BF16), pltpu.VMEM((slots, dim), BF16), pltpu.VMEM((slots, dim), BF16),
            pltpu.VMEM((n_slot, half + STAT, 128), F32), wide, pltpu.VMEM((dim, slots), BF16),
            dma((4,)), dma((rows // 128,)),
        ],
        q, k, v, bias, raw=(0, 1, 2), raw_outs=(0,), mib=62, name="forward",
    )
    got = lax.all_to_all(parts, ("chip", "core"), 0, 0)
    far = lax.ppermute(own, "query", across)
    t_own = lax.dynamic_slice_in_dim(t, chip * 128, 128, 0)
    mine, spread = call(
        combine_kernel,
        [(half + STAT, 128), (n_chip, half + STAT + 64, 128)],
        [pltpu.VMEM((dim, 128), F32)],
        got, t_own, target_lse.reshape(rows // 128, 128), far, name="combine",
    )

    def trade(x):
        return lax.all_to_all(x, "chip", 0, 0)

    near_a = trade(spread)
    theirs = lax.ppermute(mine, "query", across)
    theirs_all = jnp.broadcast_to(theirs[None], (n_chip,) + theirs.shape)
    near_a, theirs_all = lax.optimization_barrier((near_a, theirs_all))
    near_b = lax.ppermute(near_a, "core", across)
    far_a = trade(theirs_all)
    cost = pl.CostEstimate(flops=8 * rows * slots * dim, bytes_accessed=4 << 20, transcendentals=rows * slots)
    grad_s = pltpu.VMEM((dim, rows), BF16)
    mat = (slots, dim)
    gk, gv, gb, q_far, done = call(
        functools.partial(near_kernel, scale),
        [mat, mat, (slots, 128), ((rows, dim), BF16), (8, 128)],
        [wide, grad_s],
        q, near_a, near_b, k, v, bias, placed=False, cost=cost, mib=52, name="backward_near",
    )
    far_a, done = lax.optimization_barrier((far_a, done))
    far_b = lax.ppermute(far_a, "core", across)
    gk, gv, gb, sq = call(
        functools.partial(far_kernel, scale),
        [mat, mat, (1, slots), (n_chip, 128)],
        [
            pltpu.VMEM((rows, dim), BF16), pltpu.VMEM((slots, dim), BF16), pltpu.VMEM((slots, dim), BF16),
            pltpu.VMEM(mat, F32), pltpu.VMEM(mat, F32), wide, wide, grad_s, wide, dma((7,)),
        ],
        q_far, far_a, far_b, k, v, bias, gk, gv, gb, done, raw=(0, 3, 4, 6, 7, 8), cost=cost, mib=52, name="backward_far",
    )
    plane = jnp.sum(lax.all_to_all(sq.reshape(n_chip, 1, 128), "chip", 0, 0), axis=0)
    n_line = 2 * lax.axis_size("head")
    line = jnp.broadcast_to(plane[None], (n_line, 1, 128))
    sq_all = lax.all_to_all(line, ("head", "core"), 0, 0)
    counts = (float(n_all * slots * dim), float(n_all * slots * dim), float(n_all * slots))
    ok, ov, ob = call(
        functools.partial(scale_kernel, counts),
        [mat, mat, (1, slots)],
        [pltpu.VMEM(mat, F32), pltpu.VMEM(mat, F32), dma((2 * PIECES,))],
        sq_all.reshape(n_line, 128), gk, gv, gb, raw_outs=(0, 1), mib=32, name="normalize",
    )
    return ok[None], ov[None], ob


def solution(mesh):
    heads, halves, slots = (mesh.shape[name] for name in ("head", "query", "slot"))
    split = jax.sharding.Mesh(
        mesh.devices.reshape(heads, halves, slots // 2, 2), ("head", "query", "chip", "core")
    )
    slot = ("chip", "core")
    placed = (
        P("head", "query", None),
        P("head", slot, None),
        P("head", slot, None),
        P("head", slot),
        P("head", "query", None),
        P("head", "query"),
    )
    return jax.shard_map(
        local,
        mesh=split,
        in_specs=placed,
        out_specs=(P("head", slot, None), P("head", slot, None), P("head", slot)),
        check_vma=False,
    )
```

```python
import functools
import math

import jax
import jax.numpy as jnp
from jax import lax
from jax.experimental import pallas as pl
from jax.experimental.pallas import tpu as pltpu
from jax.sharding import PartitionSpec as P

EPS = 1e-06
LOG2E = math.log2(math.e)
F32 = jnp.float32
BF16 = jnp.bfloat16
MIB = 1024 * 1024
STAT = 8
PIECES = 4
SLOTS = 512
FAR_ROWS = 512
ROWS = 256


def whole(shape):
    return pl.BlockSpec(shape, lambda *_: (0,) * len(shape))


def call(kernel, outs, scratch, *args, raw=(), raw_outs=(), cost=None, mib=32, name=None, placed=True):
    outs = [o if isinstance(o[1], type) else (o, F32) for o in outs]
    anywhere = pl.BlockSpec(memory_space=pltpu.HBM)
    held = pl.BlockSpec(memory_space=pltpu.VMEM)
    return pl.pallas_call(
        kernel,
        grid=() if placed else (1,),
        out_shape=[jax.ShapeDtypeStruct(o, t) for o, t in outs],
        in_specs=[anywhere if i in raw else held if placed else whole(a.shape) for i, a in enumerate(args)],
        out_specs=[anywhere if i in raw_outs else held if placed else whole(o) for i, (o, _) in enumerate(outs)],
        scratch_shapes=scratch,
        compiler_params=pltpu.CompilerParams(vmem_limit_bytes=mib * MIB),
        cost_estimate=cost,
        name=name,
    )(*args)


def begin(pairs, sems):
    copies = [pltpu.make_async_copy(a, b, sems.at[i]) for i, (a, b) in enumerate(pairs)]
    for copy in copies:
        copy.start()
    return copies


def contract(a, b, dims):
    return lax.dot_general(a, b, ((dims[:1], dims[1:]), ((), ())), preferred_element_type=F32)


def spread_bias(bias_ref, out_ref):
    slots = bias_ref.shape[1]
    out_ref[...] = jnp.broadcast_to(bias_ref[...] * LOG2E, (128, slots)).T


def tiled_lanes(x, times):
    return jnp.concatenate([x] * times, axis=1)


def forward_piece(scale, q, k, vt, bias):
    s = contract(k, q, (1, 1)) * (scale * LOG2E) + bias
    top = jnp.max(s, axis=0, keepdims=True)
    e = jnp.exp2(s - top)
    total = jnp.sum(e, axis=0, keepdims=True)
    return top, total, contract(vt, e.astype(BF16), (1, 0))


def forward_kernel(
    scale, q_hbm, k_hbm, v_hbm, bias_ref, out_hbm, own_ref, q_ref, k_ref, v_ref, out_ref, bias_s, vt_s, sems, out_sems
):
    rows, dim = q_ref.shape
    slots = k_ref.shape[0]
    half = dim // 2
    size = min(SLOTS, slots)
    spans = [slice(i * size, (i + 1) * size) for i in range(slots // size)]
    k_copy, first_copy, v_copy, rest_copy = begin(
        [
            (k_hbm, k_ref),
            (q_hbm.at[pl.ds(0, 128)], q_ref.at[pl.ds(0, 128)]),
            (v_hbm, v_ref),
            (q_hbm.at[pl.ds(128, rows - 128)], q_ref.at[pl.ds(128, rows - 128)]),
        ],
        sems,
    )
    spread_bias(bias_ref, bias_s)
    for copy in (k_copy, first_copy, v_copy):
        copy.wait()
    vt_s[...] = v_ref[...].T
    rest_copy.wait()
    out_copies = []
    for b in range(rows // 128):
        q = q_ref[b * 128 : (b + 1) * 128, :]
        pieces = [forward_piece(scale, q, k_ref[x, :], vt_s[:, x], bias_s[x, :]) for x in spans]
        top = functools.reduce(jnp.maximum, [piece[0] for piece in pieces])
        factors = [jnp.exp2(piece[0] - top) for piece in pieces]
        total = sum(piece[1] * f for piece, f in zip(pieces, factors))
        o = sum(piece[2] * f for piece, f in zip(pieces, factors))
        for c in range(2):
            out_ref[2 * b + c, :half, :] = o[c * half : (c + 1) * half, :]
            out_ref[2 * b + c, half : half + 1, :] = top
            out_ref[2 * b + c, half + 1 : half + 2, :] = total
            out_ref[2 * b + c, half + 2 :, :] = jnp.zeros((STAT - 2, 128), F32)
        done = pl.ds(2 * b, 2)
        copy = pltpu.make_async_copy(out_ref.at[done], out_hbm.at[done], out_sems.at[b])
        copy.start()
        out_copies.append(copy)
    first = (lax.axis_index("chip") * 2 + lax.axis_index("core")) * 64
    own_ref[...] = q_ref[pl.ds(pl.multiple_of(first, 64), 64), :].astype(F32)
    for copy in out_copies:
        copy.wait()


def combine_kernel(got_ref, t_ref, tl_ref, far_ref, out_ref, all_ref, t_s):
    n = got_ref.shape[0]
    half = got_ref.shape[1] - STAT
    core = lax.axis_index("core")
    tops = got_ref[:, half, :]
    totals = got_ref[:, half + 1, :]
    top = jnp.max(tops, axis=0, keepdims=True)
    factor = jnp.exp2(tops - top)
    total = jnp.sum(totals * factor, axis=0, keepdims=True)
    summed = got_ref[0, :half, :] * factor[0:1, :]
    for i in range(1, n):
        summed += got_ref[i, :half, :] * factor[i : i + 1, :]
    outputs = summed / total
    lse2 = top + jnp.log2(total)
    t_s[...] = t_ref[...].T
    start = pl.multiple_of(core * half, half)
    grad_out = outputs - t_s[pl.ds(start, half), :]
    grad_lse = lse2 * math.log(2.0) - tl_ref[pl.ds(lax.axis_index("chip"), 1), :]
    part = jnp.sum(grad_out * outputs, axis=0, keepdims=True)
    first = jnp.where(core == 0, 1.0, 0.0).astype(F32)
    out_ref[:half, :] = grad_out
    out_ref[half : half + 1, :] = lse2
    out_ref[half + 1 : half + 2, :] = part - first * grad_lse
    out_ref[half + 2 :, :] = jnp.zeros((STAT - 2, 128), F32)
    mine = out_ref[...]
    far = far_ref[...]
    for i in range(all_ref.shape[0]):
        all_ref[i, : half + STAT, :] = mine
        all_ref[i, half + STAT :, :] = far


def gather_rows(core, ga_ref, gb_ref, half, grad_s, blocks):
    for b in blocks:
        lanes = slice(b * 128, (b + 1) * 128)
        grad_s[pl.ds(pl.multiple_of(core * half, half), half), lanes] = ga_ref[b, :half, :].astype(BF16)
        grad_s[pl.ds(pl.multiple_of((1 - core) * half, half), half), lanes] = gb_ref[b, :half, :].astype(BF16)


def backward_rows(scale, r, n, q_ref, ga_ref, gb_ref, k_ref, v_ref, bias_s, grad_s):
    half = k_ref.shape[1] // 2
    blocks = range(r * (n // 128), (r + 1) * (n // 128))
    lse2 = jnp.concatenate([ga_ref[b, half : half + 1, :] for b in blocks], axis=1)
    shift = jnp.concatenate(
        [ga_ref[b, half + 1 : half + 2, :] + gb_ref[b, half + 1 : half + 2, :] for b in blocks], axis=1
    )
    grad_out = grad_s[:, r * n : (r + 1) * n]
    q = q_ref[r * n : (r + 1) * n, :]
    s = contract(k_ref[...], q, (1, 1)) * (scale * LOG2E) + tiled_lanes(bias_s[...], n // 128)
    p = jnp.exp2(s - lse2)
    inner = contract(v_ref[...], grad_out, (1, 0))
    d = p * (inner - shift)
    gv = contract(p.astype(BF16), grad_out, (1, 1))
    gk = contract(d.astype(BF16), q, (1, 0))
    gb = d[:, :128]
    for g in range(1, n // 128):
        gb = gb + d[:, g * 128 : (g + 1) * 128]
    return gk, gv, gb


def near_kernel(
    scale, q_ref, ga_ref, gb_ref, k_ref, v_ref, bias_ref,
    gk_ref, gv_ref, gb_out_ref, far_ref, done_ref, bias_s, grad_s
):
    core = lax.axis_index("core")
    half = k_ref.shape[1] // 2
    spread_bias(bias_ref, bias_s)
    gather_rows(core, ga_ref, gb_ref, half, grad_s, range(ga_ref.shape[0]))
    skip = half + STAT
    for b in range(ga_ref.shape[0]):
        far_ref[pl.ds(pl.multiple_of(b * 128 + core * 64, 64), 64), :] = ga_ref[b, skip:, :].astype(BF16)
        far_ref[pl.ds(pl.multiple_of(b * 128 + (1 - core) * 64, 64), 64), :] = gb_ref[b, skip:, :].astype(BF16)
    done_ref[...] = jnp.zeros(done_ref.shape, F32)
    for r in range(q_ref.shape[0] // ROWS):
        gk, gv, gb = backward_rows(scale, r, ROWS, q_ref, ga_ref, gb_ref, k_ref, v_ref, bias_s, grad_s)
        if r == 0:
            gk_ref[...], gv_ref[...], gb_out_ref[...] = gk, gv, gb
        else:
            gk_ref[...] += gk
            gv_ref[...] += gv
            gb_out_ref[...] += gb


def far_kernel(
    scale, q_ref, ga_ref, gb_ref, k_ref, v_ref, bias_ref, gk0_hbm, gv0_hbm, gb0_hbm, done_ref,
    gk_ref, gv_ref, gb_out_ref, sq_ref, gk0_ref, gv0_ref, gb0_ref, bias_s, grad_s, gb_s, sems
):
    core = lax.axis_index("core")
    half = k_ref.shape[1] // 2
    slots = k_ref.shape[0]
    copies = begin([(gk0_hbm, gk0_ref), (gv0_hbm, gv0_ref), (gb0_hbm, gb0_ref)], sems)
    spread_bias(bias_ref, bias_s)
    gather_rows(core, ga_ref, gb_ref, half, grad_s, range(ga_ref.shape[0]))
    size = min(256, slots)
    step = min(FAR_ROWS, q_ref.shape[0])
    for c in range(slots // size):
        part = pl.ds(c * size, size)
        sums = None
        for r in range(q_ref.shape[0] // step):
            got = backward_rows(
                scale, r, step, q_ref, ga_ref, gb_ref, k_ref.at[part], v_ref.at[part], bias_s.at[part], grad_s
            )
            sums = got if sums is None else tuple(x + y for x, y in zip(sums, got))
        gk_ref[part, :], gv_ref[part, :], gb_s[part, :] = sums
    for copy in copies[-3:]:
        copy.wait()
    gk = (gk_ref[...] + gk0_ref[...]) * scale
    gk_ref[...] = gk
    gv = gv_ref[...] + gv0_ref[...]
    gv_ref[...] = gv
    gb = jnp.sum((gb_s[...] + gb0_ref[...]).T, axis=0, keepdims=True)
    gb_out_ref[...] = gb
    lane = lax.broadcasted_iota(jnp.int32, (1, 128), 1)
    sums = [jnp.sum(x * x) for x in (gk, gv, gb)]
    row = jnp.where(lane == 0, sums[0], jnp.where(lane == 1, sums[1], sums[2]))
    sq_ref[...] = jnp.broadcast_to(row, sq_ref.shape)


def scale_kernel(counts, sq_ref, gk_ref, gv_ref, gb_ref, ok_hbm, ov_hbm, ob_ref, sk_ref, sv_ref, sems):
    size = gk_ref.shape[0] // PIECES
    total = jnp.sum(sq_ref[...], axis=0, keepdims=True)
    lane = lax.broadcasted_iota(jnp.int32, (1, 128), 1)
    factors = []
    for i, count in enumerate(counts):
        mean = jnp.sum(jnp.where(lane == i, total, 0.0), axis=1, keepdims=True) / count
        factors.append(1.0 / jnp.sqrt(mean + EPS))
    copies = []
    for i, (g_ref, s_ref, out) in enumerate(((gk_ref, sk_ref, ok_hbm), (gv_ref, sv_ref, ov_hbm))):
        for j in range(PIECES):
            span = pl.ds(j * size, size)
            s_ref[span, :] = g_ref[span, :] * factors[i]
            copy = pltpu.make_async_copy(s_ref.at[span], out.at[span], sems.at[i * PIECES + j])
            copy.start()
            copies.append(copy)
    ob_ref[...] = gb_ref[...] * factors[2]
    for copy in copies:
        copy.wait()


def local(queries, keys, values, bias, targets, target_lse):
    q, k, v, t = queries[0], keys[0], values[0], targets[0]
    rows, dim = q.shape
    slots = k.shape[0]
    half = dim // 2
    scale = dim ** (-0.5)
    n_chip = lax.axis_size("chip")
    n_slot = 2 * n_chip
    n_all = lax.axis_size("head") * n_slot
    chip, core = lax.axis_index("chip"), lax.axis_index("core")
    dma = pltpu.SemaphoreType.DMA
    across = [(0, 1), (1, 0)]
    wide = pltpu.VMEM((slots, 128), F32)

    parts, own = call(
        functools.partial(forward_kernel, scale),
        [(n_slot, half + STAT, 128), (64, dim)],
        [
            pltpu.VMEM((rows, dim), BF16), pltpu.VMEM((slots, dim), BF16), pltpu.VMEM((slots, dim), BF16),
            pltpu.VMEM((n_slot, half + STAT, 128), F32), wide, pltpu.VMEM((dim, slots), BF16),
            dma((4,)), dma((rows // 128,)),
        ],
        q, k, v, bias, raw=(0, 1, 2), raw_outs=(0,), mib=62, name="forward",
    )
    got = lax.all_to_all(parts, ("chip", "core"), 0, 0)
    far = lax.ppermute(own, "query", across)
    t_own = lax.dynamic_slice_in_dim(t, chip * 128, 128, 0)
    mine, spread = call(
        combine_kernel,
        [(half + STAT, 128), (n_chip, half + STAT + 64, 128)],
        [pltpu.VMEM((dim, 128), F32)],
        got, t_own, target_lse.reshape(rows // 128, 128), far, name="combine",
    )

    def trade(x):
        return lax.all_to_all(x, "chip", 0, 0)

    near_a = trade(spread)
    theirs = lax.ppermute(mine, "query", across)
    theirs_all = jnp.broadcast_to(theirs[None], (n_chip,) + theirs.shape)
    near_a, theirs_all = lax.optimization_barrier((near_a, theirs_all))
    near_b = lax.ppermute(near_a, "core", across)
    far_a = trade(theirs_all)
    cost = pl.CostEstimate(flops=8 * rows * slots * dim, bytes_accessed=4 << 20, transcendentals=rows * slots)
    grad_s = pltpu.VMEM((dim, rows), BF16)
    mat = (slots, dim)
    gk, gv, gb, q_far, done = call(
        functools.partial(near_kernel, scale),
        [mat, mat, (slots, 128), ((rows, dim), BF16), (8, 128)],
        [wide, grad_s],
        q, near_a, near_b, k, v, bias, placed=False, cost=cost, mib=52, name="backward_near",
    )
    far_a, done = lax.optimization_barrier((far_a, done))
    far_b = lax.ppermute(far_a, "core", across)
    gk, gv, gb, sq = call(
        functools.partial(far_kernel, scale),
        [mat, mat, (1, slots), (n_chip, 128)],
        [
            pltpu.VMEM(mat, F32), pltpu.VMEM(mat, F32), wide, wide, grad_s, wide, dma((3,)),
        ],
        q_far, far_a, far_b, k, v, bias, gk, gv, gb, done, raw=(6, 7, 8), cost=cost, mib=52, name="backward_far",
    )
    plane = jnp.sum(lax.all_to_all(sq.reshape(n_chip, 1, 128), "chip", 0, 0), axis=0)
    n_line = 2 * lax.axis_size("head")
    line = jnp.broadcast_to(plane[None], (n_line, 1, 128))
    sq_all = lax.all_to_all(line, ("head", "core"), 0, 0)
    counts = (float(n_all * slots * dim), float(n_all * slots * dim), float(n_all * slots))
    ok, ov, ob = call(
        functools.partial(scale_kernel, counts),
        [mat, mat, (1, slots)],
        [pltpu.VMEM(mat, F32), pltpu.VMEM(mat, F32), dma((2 * PIECES,))],
        sq_all.reshape(n_line, 128), gk, gv, gb, raw_outs=(0, 1), mib=32, name="normalize",
    )
    return ok[None], ov[None], ob


def solution(mesh):
    heads, halves, slots = (mesh.shape[name] for name in ("head", "query", "slot"))
    split = jax.sharding.Mesh(
        mesh.devices.reshape(heads, halves, slots // 2, 2), ("head", "query", "chip", "core")
    )
    slot = ("chip", "core")
    placed = (
        P("head", "query", None),
        P("head", slot, None),
        P("head", slot, None),
        P("head", slot),
        P("head", "query", None),
        P("head", "query"),
    )
    return jax.shard_map(
        local,
        mesh=split,
        in_specs=placed,
        out_specs=(P("head", slot, None), P("head", slot, None), P("head", slot)),
        check_vma=False,
    )
```

```python
import functools
import math

import jax
import jax.numpy as jnp
from jax import lax
from jax.experimental import pallas as pl
from jax.experimental.pallas import tpu as pltpu
from jax.sharding import PartitionSpec as P

EPS = 1e-06
LOG2E = math.log2(math.e)
F32 = jnp.float32
BF16 = jnp.bfloat16
MIB = 1024 * 1024
STAT = 8
PIECES = 4
SLOTS = 512
FAR_ROWS = 512
ROWS = 256


def whole(shape):
    return pl.BlockSpec(shape, lambda *_: (0,) * len(shape))


def call(kernel, outs, scratch, *args, raw=(), raw_outs=(), cost=None, mib=32, name=None, placed=True):
    outs = [o if isinstance(o[1], type) else (o, F32) for o in outs]
    anywhere = pl.BlockSpec(memory_space=pltpu.HBM)
    held = pl.BlockSpec(memory_space=pltpu.VMEM)
    return pl.pallas_call(
        kernel,
        grid=() if placed else (1,),
        out_shape=[jax.ShapeDtypeStruct(o, t) for o, t in outs],
        in_specs=[anywhere if i in raw else held if placed else whole(a.shape) for i, a in enumerate(args)],
        out_specs=[anywhere if i in raw_outs else held if placed else whole(o) for i, (o, _) in enumerate(outs)],
        scratch_shapes=scratch,
        compiler_params=pltpu.CompilerParams(vmem_limit_bytes=mib * MIB),
        cost_estimate=cost,
        name=name,
    )(*args)


def begin(pairs, sems):
    copies = [pltpu.make_async_copy(a, b, sems.at[i]) for i, (a, b) in enumerate(pairs)]
    for copy in copies:
        copy.start()
    return copies


def contract(a, b, dims):
    return lax.dot_general(a, b, ((dims[:1], dims[1:]), ((), ())), preferred_element_type=F32)


def spread_bias(bias_ref, out_ref):
    slots = bias_ref.shape[1]
    out_ref[...] = jnp.broadcast_to(bias_ref[...] * LOG2E, (128, slots)).T


def tiled_lanes(x, times):
    return jnp.concatenate([x] * times, axis=1)


def forward_piece(scale, q, k, vt, bias):
    s = contract(k, q, (1, 1)) * (scale * LOG2E) + bias
    top = jnp.max(s, axis=0, keepdims=True)
    e = jnp.exp2(s - top)
    total = jnp.sum(e, axis=0, keepdims=True)
    return top, total, contract(vt, e.astype(BF16), (1, 0))


def forward_kernel(
    scale, q_hbm, k_hbm, v_hbm, bias_hbm, out_hbm, own_hbm,
    q_ref, k_ref, v_ref, bias_ref, out_ref, own_ref, bias_s, vt_s, sems, out_sems
):
    rows, dim = q_ref.shape
    slots = k_ref.shape[0]
    half = dim // 2
    size = min(SLOTS, slots)
    spans = [slice(i * size, (i + 1) * size) for i in range(slots // size)]
    copies = begin([(bias_hbm, bias_ref), (v_hbm, v_ref), (k_hbm, k_ref), (q_hbm, q_ref)], sems)
    copies[0].wait()
    spread_bias(bias_ref, bias_s)
    copies[1].wait()
    vt_s[...] = v_ref[...].T
    copies[2].wait()
    copies[3].wait()
    first = (lax.axis_index("chip") * 2 + lax.axis_index("core")) * 64
    own_ref[...] = q_ref[pl.ds(pl.multiple_of(first, 64), 64), :].astype(F32)
    own_copy = pltpu.make_async_copy(own_ref, own_hbm, out_sems.at[rows // 128])
    own_copy.start()
    out_copies = []
    for b in range(rows // 128):
        q = q_ref[b * 128 : (b + 1) * 128, :]
        pieces = [forward_piece(scale, q, k_ref[x, :], vt_s[:, x], bias_s[x, :]) for x in spans]
        top = functools.reduce(jnp.maximum, [piece[0] for piece in pieces])
        factors = [jnp.exp2(piece[0] - top) for piece in pieces]
        total = sum(piece[1] * f for piece, f in zip(pieces, factors))
        o = sum(piece[2] * f for piece, f in zip(pieces, factors))
        for c in range(2):
            out_ref[2 * b + c, :half, :] = o[c * half : (c + 1) * half, :]
            out_ref[2 * b + c, half : half + 1, :] = top
            out_ref[2 * b + c, half + 1 : half + 2, :] = total
            out_ref[2 * b + c, half + 2 :, :] = jnp.zeros((STAT - 2, 128), F32)
        done = pl.ds(2 * b, 2)
        copy = pltpu.make_async_copy(out_ref.at[done], out_hbm.at[done], out_sems.at[b])
        copy.start()
        out_copies.append(copy)
    own_copy.wait()
    for copy in out_copies:
        copy.wait()


def combine_kernel(got_ref, t_ref, tl_ref, far_ref, out_ref, all_hbm, t_s, one_ref, sems):
    n = got_ref.shape[0]
    half = got_ref.shape[1] - STAT
    core = lax.axis_index("core")
    tops = got_ref[:, half, :]
    totals = got_ref[:, half + 1, :]
    top = jnp.max(tops, axis=0, keepdims=True)
    factor = jnp.exp2(tops - top)
    total = jnp.sum(totals * factor, axis=0, keepdims=True)
    summed = got_ref[0, :half, :] * factor[0:1, :]
    for i in range(1, n):
        summed += got_ref[i, :half, :] * factor[i : i + 1, :]
    outputs = summed / total
    lse2 = top + jnp.log2(total)
    t_s[...] = t_ref[...].T
    start = pl.multiple_of(core * half, half)
    grad_out = outputs - t_s[pl.ds(start, half), :]
    grad_lse = lse2 * math.log(2.0) - tl_ref[pl.ds(lax.axis_index("chip"), 1), :]
    part = jnp.sum(grad_out * outputs, axis=0, keepdims=True)
    first = jnp.where(core == 0, 1.0, 0.0).astype(F32)
    out_ref[:half, :] = grad_out
    out_ref[half : half + 1, :] = lse2
    out_ref[half + 1 : half + 2, :] = part - first * grad_lse
    out_ref[half + 2 :, :] = jnp.zeros((STAT - 2, 128), F32)
    one_ref[: half + STAT, :] = out_ref[...]
    one_ref[half + STAT :, :] = far_ref[...]
    copies = begin([(one_ref, all_hbm.at[i]) for i in range(all_hbm.shape[0])], sems)
    for copy in copies:
        copy.wait()


def gather_rows(core, ga_ref, gb_ref, half, grad_s, blocks):
    for b in blocks:
        lanes = slice(b * 128, (b + 1) * 128)
        grad_s[pl.ds(pl.multiple_of(core * half, half), half), lanes] = ga_ref[b, :half, :].astype(BF16)
        grad_s[pl.ds(pl.multiple_of((1 - core) * half, half), half), lanes] = gb_ref[b, :half, :].astype(BF16)


def backward_rows(scale, r, n, q_ref, ga_ref, gb_ref, k_ref, v_ref, bias_s, grad_s):
    half = k_ref.shape[1] // 2
    blocks = range(r * (n // 128), (r + 1) * (n // 128))
    lse2 = jnp.concatenate([ga_ref[b, half : half + 1, :] for b in blocks], axis=1)
    shift = jnp.concatenate(
        [ga_ref[b, half + 1 : half + 2, :] + gb_ref[b, half + 1 : half + 2, :] for b in blocks], axis=1
    )
    grad_out = grad_s[:, r * n : (r + 1) * n]
    q = q_ref[r * n : (r + 1) * n, :]
    s = contract(k_ref[...], q, (1, 1)) * (scale * LOG2E) + tiled_lanes(bias_s[...], n // 128)
    p = jnp.exp2(s - lse2)
    inner = contract(v_ref[...], grad_out, (1, 0))
    d = p * (inner - shift)
    gv = contract(p.astype(BF16), grad_out, (1, 1))
    gk = contract(d.astype(BF16), q, (1, 0))
    gb = d[:, :128]
    for g in range(1, n // 128):
        gb = gb + d[:, g * 128 : (g + 1) * 128]
    return gk, gv, gb


def near_kernel(
    scale, q_ref, ga_ref, gb_ref, k_ref, v_ref, bias_ref,
    gk_ref, gv_ref, gb_out_ref, far_ref, done_ref, bias_s, grad_s
):
    core = lax.axis_index("core")
    half = k_ref.shape[1] // 2
    spread_bias(bias_ref, bias_s)
    gather_rows(core, ga_ref, gb_ref, half, grad_s, range(ga_ref.shape[0]))
    skip = half + STAT
    for b in range(ga_ref.shape[0]):
        far_ref[pl.ds(pl.multiple_of(b * 128 + core * 64, 64), 64), :] = ga_ref[b, skip:, :].astype(BF16)
        far_ref[pl.ds(pl.multiple_of(b * 128 + (1 - core) * 64, 64), 64), :] = gb_ref[b, skip:, :].astype(BF16)
    done_ref[...] = jnp.zeros(done_ref.shape, F32)
    for r in range(q_ref.shape[0] // ROWS):
        gk, gv, gb = backward_rows(scale, r, ROWS, q_ref, ga_ref, gb_ref, k_ref, v_ref, bias_s, grad_s)
        if r == 0:
            gk_ref[...], gv_ref[...], gb_out_ref[...] = gk, gv, gb
        else:
            gk_ref[...] += gk
            gv_ref[...] += gv
            gb_out_ref[...] += gb


def far_kernel(
    scale, q_ref, ga_ref, gb_ref, k_ref, v_ref, bias_ref, gk0_hbm, gv0_hbm, gb0_hbm, done_ref,
    gk_ref, gv_ref, gb_out_ref, sq_ref, gk0_ref, gv0_ref, gb0_ref, bias_s, grad_s, gb_s, sems
):
    core = lax.axis_index("core")
    half = k_ref.shape[1] // 2
    slots = k_ref.shape[0]
    copies = begin([(gk0_hbm, gk0_ref), (gv0_hbm, gv0_ref), (gb0_hbm, gb0_ref)], sems)
    spread_bias(bias_ref, bias_s)
    gather_rows(core, ga_ref, gb_ref, half, grad_s, range(ga_ref.shape[0]))
    size = min(256, slots)
    step = min(FAR_ROWS, q_ref.shape[0])
    for c in range(slots // size):
        part = pl.ds(c * size, size)
        sums = None
        for r in range(q_ref.shape[0] // step):
            got = backward_rows(
                scale, r, step, q_ref, ga_ref, gb_ref, k_ref.at[part], v_ref.at[part], bias_s.at[part], grad_s
            )
            sums = got if sums is None else tuple(x + y for x, y in zip(sums, got))
        gk_ref[part, :], gv_ref[part, :], gb_s[part, :] = sums
    for copy in copies[-3:]:
        copy.wait()
    gk = (gk_ref[...] + gk0_ref[...]) * scale
    gk_ref[...] = gk
    gv = gv_ref[...] + gv0_ref[...]
    gv_ref[...] = gv
    gb = jnp.sum((gb_s[...] + gb0_ref[...]).T, axis=0, keepdims=True)
    gb_out_ref[...] = gb
    lane = lax.broadcasted_iota(jnp.int32, (1, 128), 1)
    sums = [jnp.sum(x * x) for x in (gk, gv, gb)]
    row = jnp.where(lane == 0, sums[0], jnp.where(lane == 1, sums[1], sums[2]))
    sq_ref[...] = jnp.broadcast_to(row, sq_ref.shape)


def scale_kernel(counts, sq_ref, gk_ref, gv_ref, gb_ref, ok_hbm, ov_hbm, ob_hbm, sk_ref, sv_ref, sb_ref, sems):
    size = gk_ref.shape[0] // PIECES
    total = jnp.sum(sq_ref[...], axis=0, keepdims=True)
    lane = lax.broadcasted_iota(jnp.int32, (1, 128), 1)
    factors = []
    for i, count in enumerate(counts):
        mean = jnp.sum(jnp.where(lane == i, total, 0.0), axis=1, keepdims=True) / count
        factors.append(1.0 / jnp.sqrt(mean + EPS))
    sb_ref[...] = gb_ref[...] * factors[2]
    copies = [pltpu.make_async_copy(sb_ref, ob_hbm, sems.at[2 * PIECES])]
    copies[0].start()
    for i, (g_ref, s_ref, out) in enumerate(((gk_ref, sk_ref, ok_hbm), (gv_ref, sv_ref, ov_hbm))):
        for j in range(PIECES):
            span = pl.ds(j * size, size)
            s_ref[span, :] = g_ref[span, :] * factors[i]
            copy = pltpu.make_async_copy(s_ref.at[span], out.at[span], sems.at[i * PIECES + j])
            copy.start()
            copies.append(copy)
    for copy in copies:
        copy.wait()


def local(queries, keys, values, bias, targets, target_lse):
    q, k, v, t = queries[0], keys[0], values[0], targets[0]
    rows, dim = q.shape
    slots = k.shape[0]
    half = dim // 2
    scale = dim ** (-0.5)
    n_chip = lax.axis_size("chip")
    n_slot = 2 * n_chip
    n_all = lax.axis_size("head") * n_slot
    chip, core = lax.axis_index("chip"), lax.axis_index("core")
    dma = pltpu.SemaphoreType.DMA
    across = [(0, 1), (1, 0)]
    wide = pltpu.VMEM((slots, 128), F32)

    parts, own = call(
        functools.partial(forward_kernel, scale),
        [(n_slot, half + STAT, 128), (64, dim)],
        [
            pltpu.VMEM((rows, dim), BF16), pltpu.VMEM((slots, dim), BF16), pltpu.VMEM((slots, dim), BF16),
            pltpu.VMEM((1, slots), F32), pltpu.VMEM((n_slot, half + STAT, 128), F32), pltpu.VMEM((64, dim), F32),
            wide, pltpu.VMEM((dim, slots), BF16), dma((4,)), dma((rows // 128 + 1,)),
        ],
        q, k, v, bias, raw=(0, 1, 2, 3), raw_outs=(0, 1), mib=62, name="forward",
    )
    got = lax.all_to_all(parts, ("chip", "core"), 0, 0)
    far = lax.ppermute(own, "query", across)
    t_own = lax.dynamic_slice_in_dim(t, chip * 128, 128, 0)
    mine, spread = call(
        combine_kernel,
        [(half + STAT, 128), (n_chip, half + STAT + 64, 128)],
        [pltpu.VMEM((dim, 128), F32), pltpu.VMEM((half + STAT + 64, 128), F32), dma((n_chip,))],
        got, t_own, target_lse.reshape(rows // 128, 128), far, raw_outs=(1,), name="combine",
    )

    def trade(x):
        return lax.all_to_all(x, "chip", 0, 0)

    near_a = trade(spread)
    theirs = lax.ppermute(mine, "query", across)
    theirs_all = jnp.broadcast_to(theirs[None], (n_chip,) + theirs.shape)
    near_a, theirs_all = lax.optimization_barrier((near_a, theirs_all))
    near_b = lax.ppermute(near_a, "core", across)
    far_a = trade(theirs_all)
    cost = pl.CostEstimate(flops=8 * rows * slots * dim, bytes_accessed=4 << 20, transcendentals=rows * slots)
    grad_s = pltpu.VMEM((dim, rows), BF16)
    mat = (slots, dim)
    gk, gv, gb, q_far, done = call(
        functools.partial(near_kernel, scale),
        [mat, mat, (slots, 128), ((rows, dim), BF16), (8, 128)],
        [wide, grad_s],
        q, near_a, near_b, k, v, bias, placed=False, cost=cost, mib=52, name="backward_near",
    )
    far_a, done = lax.optimization_barrier((far_a, done))
    far_b = lax.ppermute(far_a, "core", across)
    gk, gv, gb, sq = call(
        functools.partial(far_kernel, scale),
        [mat, mat, (1, slots), (n_chip, 128)],
        [
            pltpu.VMEM(mat, F32), pltpu.VMEM(mat, F32), wide, wide, grad_s, wide, dma((3,)),
        ],
        q_far, far_a, far_b, k, v, bias, gk, gv, gb, done, raw=(6, 7, 8), cost=cost, mib=52, name="backward_far",
    )
    plane = jnp.sum(lax.all_to_all(sq.reshape(n_chip, 1, 128), "chip", 0, 0), axis=0)
    n_line = 2 * lax.axis_size("head")
    line = jnp.broadcast_to(plane[None], (n_line, 1, 128))
    sq_all = lax.all_to_all(line, ("head", "core"), 0, 0)
    counts = (float(n_all * slots * dim), float(n_all * slots * dim), float(n_all * slots))
    ok, ov, ob = call(
        functools.partial(scale_kernel, counts),
        [mat, mat, (1, slots)],
        [pltpu.VMEM(mat, F32), pltpu.VMEM(mat, F32), pltpu.VMEM((1, slots), F32), dma((2 * PIECES + 1,))],
        sq_all.reshape(n_line, 128), gk, gv, gb, raw_outs=(0, 1, 2), mib=32, name="normalize",
    )
    return ok[None], ov[None], ob


def solution(mesh):
    heads, halves, slots = (mesh.shape[name] for name in ("head", "query", "slot"))
    split = jax.sharding.Mesh(
        mesh.devices.reshape(heads, halves, slots // 2, 2), ("head", "query", "chip", "core")
    )
    slot = ("chip", "core")
    placed = (
        P("head", "query", None),
        P("head", slot, None),
        P("head", slot, None),
        P("head", slot),
        P("head", "query", None),
        P("head", "query"),
    )
    return jax.shard_map(
        local,
        mesh=split,
        in_specs=placed,
        out_specs=(P("head", slot, None), P("head", slot, None), P("head", slot)),
        check_vma=False,
    )
```

```python
import functools
import math

import jax
import jax.numpy as jnp
from jax import lax
from jax.experimental import pallas as pl
from jax.experimental.pallas import tpu as pltpu
from jax.sharding import PartitionSpec as P

EPS = 1e-06
LOG2E = math.log2(math.e)
F32 = jnp.float32
BF16 = jnp.bfloat16
MIB = 1024 * 1024
STAT = 8
PIECES = 4
SLOTS = 512
FAR_ROWS = 512
ROWS = 256


def whole(shape):
    return pl.BlockSpec(shape, lambda *_: (0,) * len(shape))


def call(kernel, outs, scratch, *args, raw=(), raw_outs=(), cost=None, mib=32, name=None, placed=True):
    outs = [o if isinstance(o[1], type) else (o, F32) for o in outs]
    anywhere = pl.BlockSpec(memory_space=pltpu.HBM)
    held = pl.BlockSpec(memory_space=pltpu.VMEM)
    return pl.pallas_call(
        kernel,
        grid=() if placed else (1,),
        out_shape=[jax.ShapeDtypeStruct(o, t) for o, t in outs],
        in_specs=[anywhere if i in raw else held if placed else whole(a.shape) for i, a in enumerate(args)],
        out_specs=[anywhere if i in raw_outs else held if placed else whole(o) for i, (o, _) in enumerate(outs)],
        scratch_shapes=scratch,
        compiler_params=pltpu.CompilerParams(vmem_limit_bytes=mib * MIB),
        cost_estimate=cost,
        name=name,
    )(*args)


def begin(pairs, sems):
    copies = [pltpu.make_async_copy(a, b, sems.at[i]) for i, (a, b) in enumerate(pairs)]
    for copy in copies:
        copy.start()
    return copies


def contract(a, b, dims):
    return lax.dot_general(a, b, ((dims[:1], dims[1:]), ((), ())), preferred_element_type=F32)


def spread_bias(bias_ref, out_ref):
    slots = bias_ref.shape[1]
    out_ref[...] = jnp.broadcast_to(bias_ref[...] * LOG2E, (128, slots)).T


def tiled_lanes(x, times):
    return jnp.concatenate([x] * times, axis=1)


def forward_piece(scale, q, k, vt, bias):
    s = contract(k, q, (1, 1)) * (scale * LOG2E) + bias
    top = jnp.max(s, axis=0, keepdims=True)
    e = jnp.exp2(s - top)
    total = jnp.sum(e, axis=0, keepdims=True)
    return top, total, contract(vt, e.astype(BF16), (1, 0))


def forward_kernel(
    scale, q_hbm, k_hbm, v_hbm, bias_hbm, out_hbm, own_hbm,
    q_ref, k_ref, v_ref, bias_ref, out_ref, own_ref, bias_s, vt_s, sems, out_sems
):
    rows, dim = q_ref.shape
    slots = k_ref.shape[0]
    half = dim // 2
    size = min(SLOTS, slots)
    spans = [slice(i * size, (i + 1) * size) for i in range(slots // size)]
    copies = begin([(bias_hbm, bias_ref), (v_hbm, v_ref), (k_hbm, k_ref), (q_hbm, q_ref)], sems)
    copies[0].wait()
    spread_bias(bias_ref, bias_s)
    copies[1].wait()
    vt_s[...] = v_ref[...].T
    copies[2].wait()
    copies[3].wait()
    first = (lax.axis_index("chip") * 2 + lax.axis_index("core")) * 64
    own_ref[...] = q_ref[pl.ds(pl.multiple_of(first, 64), 64), :].astype(F32)
    own_copy = pltpu.make_async_copy(own_ref, own_hbm, out_sems.at[rows // 128])
    own_copy.start()
    out_copies = []
    for b in range(rows // 128):
        q = q_ref[b * 128 : (b + 1) * 128, :]
        pieces = [forward_piece(scale, q, k_ref[x, :], vt_s[:, x], bias_s[x, :]) for x in spans]
        top = functools.reduce(jnp.maximum, [piece[0] for piece in pieces])
        factors = [jnp.exp2(piece[0] - top) for piece in pieces]
        total = sum(piece[1] * f for piece, f in zip(pieces, factors))
        o = sum(piece[2] * f for piece, f in zip(pieces, factors))
        for c in range(2):
            out_ref[2 * b + c, :half, :] = o[c * half : (c + 1) * half, :]
            out_ref[2 * b + c, half : half + 1, :] = top
            out_ref[2 * b + c, half + 1 : half + 2, :] = total
            out_ref[2 * b + c, half + 2 :, :] = jnp.zeros((STAT - 2, 128), F32)
        done = pl.ds(2 * b, 2)
        copy = pltpu.make_async_copy(out_ref.at[done], out_hbm.at[done], out_sems.at[b])
        copy.start()
        out_copies.append(copy)
    own_copy.wait()
    for copy in out_copies:
        copy.wait()


def combine_kernel(got_ref, t_ref, tl_ref, far_ref, out_ref, all_hbm, t_s, one_ref, sems):
    n = got_ref.shape[0]
    half = got_ref.shape[1] - STAT
    core = lax.axis_index("core")
    tops = got_ref[:, half, :]
    totals = got_ref[:, half + 1, :]
    top = jnp.max(tops, axis=0, keepdims=True)
    factor = jnp.exp2(tops - top)
    total = jnp.sum(totals * factor, axis=0, keepdims=True)
    summed = got_ref[0, :half, :] * factor[0:1, :]
    for i in range(1, n):
        summed += got_ref[i, :half, :] * factor[i : i + 1, :]
    outputs = summed / total
    lse2 = top + jnp.log2(total)
    t_s[...] = t_ref[...].T
    start = pl.multiple_of(core * half, half)
    grad_out = outputs - t_s[pl.ds(start, half), :]
    grad_lse = lse2 * math.log(2.0) - tl_ref[pl.ds(lax.axis_index("chip"), 1), :]
    part = jnp.sum(grad_out * outputs, axis=0, keepdims=True)
    first = jnp.where(core == 0, 1.0, 0.0).astype(F32)
    out_ref[:half, :] = grad_out
    out_ref[half : half + 1, :] = lse2
    out_ref[half + 1 : half + 2, :] = part - first * grad_lse
    out_ref[half + 2 :, :] = jnp.zeros((STAT - 2, 128), F32)
    one_ref[: half + STAT, :] = out_ref[...]
    one_ref[half + STAT :, :] = far_ref[...]
    copies = begin([(one_ref, all_hbm.at[i]) for i in range(all_hbm.shape[0])], sems)
    for copy in copies:
        copy.wait()


def gather_rows(core, ga_ref, gb_ref, half, grad_s, blocks):
    for b in blocks:
        lanes = slice(b * 128, (b + 1) * 128)
        grad_s[pl.ds(pl.multiple_of(core * half, half), half), lanes] = ga_ref[b, :half, :].astype(BF16)
        grad_s[pl.ds(pl.multiple_of((1 - core) * half, half), half), lanes] = gb_ref[b, :half, :].astype(BF16)


def backward_rows(scale, r, n, q_ref, ga_ref, gb_ref, k_ref, v_ref, bias_s, grad_s):
    half = k_ref.shape[1] // 2
    blocks = range(r * (n // 128), (r + 1) * (n // 128))
    lse2 = jnp.concatenate([ga_ref[b, half : half + 1, :] for b in blocks], axis=1)
    shift = jnp.concatenate(
        [ga_ref[b, half + 1 : half + 2, :] + gb_ref[b, half + 1 : half + 2, :] for b in blocks], axis=1
    )
    grad_out = grad_s[:, r * n : (r + 1) * n]
    q = q_ref[r * n : (r + 1) * n, :]
    s = contract(k_ref[...], q, (1, 1)) * (scale * LOG2E) + tiled_lanes(bias_s[...], n // 128)
    p = jnp.exp2(s - lse2)
    inner = contract(v_ref[...], grad_out, (1, 0))
    d = p * (inner - shift)
    gv = contract(p.astype(BF16), grad_out, (1, 1))
    gk = contract(d.astype(BF16), q, (1, 0))
    gb = d[:, :128]
    for g in range(1, n // 128):
        gb = gb + d[:, g * 128 : (g + 1) * 128]
    return gk, gv, gb


def near_kernel(
    scale, q_ref, ga_ref, gb_ref, k_ref, v_ref, bias_ref,
    gk_ref, gv_ref, gb_out_ref, far_ref, done_ref, bias_s, grad_s
):
    core = lax.axis_index("core")
    half = k_ref.shape[1] // 2
    spread_bias(bias_ref, bias_s)
    gather_rows(core, ga_ref, gb_ref, half, grad_s, range(ga_ref.shape[0]))
    skip = half + STAT
    for b in range(ga_ref.shape[0]):
        far_ref[pl.ds(pl.multiple_of(b * 128 + core * 64, 64), 64), :] = ga_ref[b, skip:, :].astype(BF16)
        far_ref[pl.ds(pl.multiple_of(b * 128 + (1 - core) * 64, 64), 64), :] = gb_ref[b, skip:, :].astype(BF16)
    done_ref[...] = jnp.zeros(done_ref.shape, F32)
    for r in range(q_ref.shape[0] // ROWS):
        gk, gv, gb = backward_rows(scale, r, ROWS, q_ref, ga_ref, gb_ref, k_ref, v_ref, bias_s, grad_s)
        if r == 0:
            gk_ref[...], gv_ref[...], gb_out_ref[...] = gk, gv, gb
        else:
            gk_ref[...] += gk
            gv_ref[...] += gv
            gb_out_ref[...] += gb


def far_kernel(
    scale, q_hbm, ga_ref, gb_ref, k_ref, v_ref, bias_ref, gk0_hbm, gv0_hbm, gb0_hbm, done_ref,
    gk_ref, gv_ref, gb_out_ref, sq_ref, q_ref, gk0_ref, gv0_ref, gb0_ref, bias_s, grad_s, gb_s, sems
):
    core = lax.axis_index("core")
    half = k_ref.shape[1] // 2
    slots = k_ref.shape[0]
    copies = begin([(q_hbm, q_ref), (gk0_hbm, gk0_ref), (gv0_hbm, gv0_ref), (gb0_hbm, gb0_ref)], sems)
    spread_bias(bias_ref, bias_s)
    gather_rows(core, ga_ref, gb_ref, half, grad_s, range(ga_ref.shape[0]))
    copies[0].wait()
    size = min(256, slots)
    step = min(FAR_ROWS, q_ref.shape[0])
    for c in range(slots // size):
        part = pl.ds(c * size, size)
        sums = None
        for r in range(q_ref.shape[0] // step):
            got = backward_rows(
                scale, r, step, q_ref, ga_ref, gb_ref, k_ref.at[part], v_ref.at[part], bias_s.at[part], grad_s
            )
            sums = got if sums is None else tuple(x + y for x, y in zip(sums, got))
        gk_ref[part, :], gv_ref[part, :], gb_s[part, :] = sums
    for copy in copies[-3:]:
        copy.wait()
    gk = (gk_ref[...] + gk0_ref[...]) * scale
    gk_ref[...] = gk
    gv = gv_ref[...] + gv0_ref[...]
    gv_ref[...] = gv
    gb = jnp.sum((gb_s[...] + gb0_ref[...]).T, axis=0, keepdims=True)
    gb_out_ref[...] = gb
    lane = lax.broadcasted_iota(jnp.int32, (1, 128), 1)
    sums = [jnp.sum(x * x) for x in (gk, gv, gb)]
    row = jnp.where(lane == 0, sums[0], jnp.where(lane == 1, sums[1], sums[2]))
    sq_ref[...] = jnp.broadcast_to(row, sq_ref.shape)


def scale_kernel(counts, sq_ref, gk_ref, gv_ref, gb_ref, ok_hbm, ov_hbm, ob_hbm, sk_ref, sv_ref, sb_ref, sems):
    size = gk_ref.shape[0] // PIECES
    total = jnp.sum(sq_ref[...], axis=0, keepdims=True)
    lane = lax.broadcasted_iota(jnp.int32, (1, 128), 1)
    factors = []
    for i, count in enumerate(counts):
        mean = jnp.sum(jnp.where(lane == i, total, 0.0), axis=1, keepdims=True) / count
        factors.append(1.0 / jnp.sqrt(mean + EPS))
    sb_ref[...] = gb_ref[...] * factors[2]
    copies = [pltpu.make_async_copy(sb_ref, ob_hbm, sems.at[2 * PIECES])]
    copies[0].start()
    for i, (g_ref, s_ref, out) in enumerate(((gk_ref, sk_ref, ok_hbm), (gv_ref, sv_ref, ov_hbm))):
        for j in range(PIECES):
            span = pl.ds(j * size, size)
            s_ref[span, :] = g_ref[span, :] * factors[i]
            copy = pltpu.make_async_copy(s_ref.at[span], out.at[span], sems.at[i * PIECES + j])
            copy.start()
            copies.append(copy)
    for copy in copies:
        copy.wait()


def local(queries, keys, values, bias, targets, target_lse):
    q, k, v, t = queries[0], keys[0], values[0], targets[0]
    rows, dim = q.shape
    slots = k.shape[0]
    half = dim // 2
    scale = dim ** (-0.5)
    n_chip = lax.axis_size("chip")
    n_slot = 2 * n_chip
    n_all = lax.axis_size("head") * n_slot
    chip, core = lax.axis_index("chip"), lax.axis_index("core")
    dma = pltpu.SemaphoreType.DMA
    across = [(0, 1), (1, 0)]
    wide = pltpu.VMEM((slots, 128), F32)

    parts, own = call(
        functools.partial(forward_kernel, scale),
        [(n_slot, half + STAT, 128), (64, dim)],
        [
            pltpu.VMEM((rows, dim), BF16), pltpu.VMEM((slots, dim), BF16), pltpu.VMEM((slots, dim), BF16),
            pltpu.VMEM((1, slots), F32), pltpu.VMEM((n_slot, half + STAT, 128), F32), pltpu.VMEM((64, dim), F32),
            wide, pltpu.VMEM((dim, slots), BF16), dma((4,)), dma((rows // 128 + 1,)),
        ],
        q, k, v, bias, raw=(0, 1, 2, 3), raw_outs=(0, 1), mib=62, name="forward",
    )
    got = lax.all_to_all(parts, ("chip", "core"), 0, 0)
    far = lax.ppermute(own, "query", across)
    t_own = lax.dynamic_slice_in_dim(t, chip * 128, 128, 0)
    mine, spread = call(
        combine_kernel,
        [(half + STAT, 128), (n_chip, half + STAT + 64, 128)],
        [pltpu.VMEM((dim, 128), F32), pltpu.VMEM((half + STAT + 64, 128), F32), dma((n_chip,))],
        got, t_own, target_lse.reshape(rows // 128, 128), far, raw_outs=(1,), name="combine",
    )

    def trade(x):
        return lax.all_to_all(x, "chip", 0, 0)

    near_a = trade(spread)
    theirs = lax.ppermute(mine, "query", across)
    theirs_all = jnp.broadcast_to(theirs[None], (n_chip,) + theirs.shape)
    near_a, theirs_all = lax.optimization_barrier((near_a, theirs_all))
    near_b = lax.ppermute(near_a, "core", across)
    far_a = trade(theirs_all)
    cost = pl.CostEstimate(flops=8 * rows * slots * dim, bytes_accessed=4 << 20, transcendentals=rows * slots)
    grad_s = pltpu.VMEM((dim, rows), BF16)
    mat = (slots, dim)
    gk, gv, gb, q_far, done = call(
        functools.partial(near_kernel, scale),
        [mat, mat, (slots, 128), ((rows, dim), BF16), (8, 128)],
        [wide, grad_s],
        q, near_a, near_b, k, v, bias, placed=False, cost=cost, mib=52, name="backward_near",
    )
    far_a, done = lax.optimization_barrier((far_a, done))
    far_b = lax.ppermute(far_a, "core", across)
    gk, gv, gb, sq = call(
        functools.partial(far_kernel, scale),
        [mat, mat, (1, slots), (n_chip, 128)],
        [
            pltpu.VMEM((rows, dim), BF16), pltpu.VMEM(mat, F32), pltpu.VMEM(mat, F32), wide, wide, grad_s, wide, dma((4,)),
        ],
        q_far, far_a, far_b, k, v, bias, gk, gv, gb, done, raw=(0, 6, 7, 8), cost=cost, mib=52, name="backward_far",
    )
    plane = jnp.sum(lax.all_to_all(sq.reshape(n_chip, 1, 128), "chip", 0, 0), axis=0)
    n_line = 2 * lax.axis_size("head")
    line = jnp.broadcast_to(plane[None], (n_line, 1, 128))
    sq_all = lax.all_to_all(line, ("head", "core"), 0, 0)
    counts = (float(n_all * slots * dim), float(n_all * slots * dim), float(n_all * slots))
    ok, ov, ob = call(
        functools.partial(scale_kernel, counts),
        [mat, mat, (1, slots)],
        [pltpu.VMEM(mat, F32), pltpu.VMEM(mat, F32), pltpu.VMEM((1, slots), F32), dma((2 * PIECES + 1,))],
        sq_all.reshape(n_line, 128), gk, gv, gb, raw_outs=(0, 1, 2), mib=32, name="normalize",
    )
    return ok[None], ov[None], ob


def solution(mesh):
    heads, halves, slots = (mesh.shape[name] for name in ("head", "query", "slot"))
    split = jax.sharding.Mesh(
        mesh.devices.reshape(heads, halves, slots // 2, 2), ("head", "query", "chip", "core")
    )
    slot = ("chip", "core")
    placed = (
        P("head", "query", None),
        P("head", slot, None),
        P("head", slot, None),
        P("head", slot),
        P("head", "query", None),
        P("head", "query"),
    )
    return jax.shard_map(
        local,
        mesh=split,
        in_specs=placed,
        out_specs=(P("head", slot, None), P("head", slot, None), P("head", slot)),
        check_vma=False,
    )
```
